256 devices in a mesh: dp: 64 (over z, x, core), branch: 4 (over y).
Axes of the slice: x: 4, y: 4, z: 8, core: 2. Of those that a mesh axis runs over, the one named last changes fastest.
Arguments:
- prefix_keys: bfloat16 [64, 4, 512, 512], P('dp', 'branch'), may hold values from -6 to 6
- prefix_values: bfloat16 [64, 4, 512, 512], P('dp', 'branch'), may hold values from -6 to 6
- resp_query: bfloat16 [64, 4, 8, 32, 4096], P('dp', 'branch'), may hold values from -6 to 6
- resp_keys: bfloat16 [64, 4, 8, 32, 512], P('dp', 'branch'), may hold values from -6 to 6
- resp_values: bfloat16 [64, 4, 8, 32, 512], P('dp', 'branch'), may hold values from -6 to 6
- out_grad: bfloat16 [64, 4, 8, 32, 4096], P('dp', 'branch'), may hold values from -6 to 6
- q_gain: float32 [128], replicated, may hold values from 0.1 to 1.9
- k_gain: float32 [128], replicated, may hold values from 0.1 to 1.9
- lengths: int32 [64, 4, 8], P('dp', 'branch'), may hold values from 1 to 32, as said below
- slot_prompt: int32 [64, 4, 8], P('dp', 'branch'), may hold values from 0 to 3, as said below
- prefix_owner: int32 [64, 4], P('dp'), may hold values from 0 to 3, as said below
Outputs:
- attended: bfloat16 [64, 4, 8, 32, 4096], P('dp', 'branch')
- d_query: bfloat16 [64, 4, 8, 32, 4096], P('dp', 'branch')
- d_resp_keys: bfloat16 [64, 4, 8, 32, 512], P('dp', 'branch')
- d_resp_values: bfloat16 [64, 4, 8, 32, 512], P('dp', 'branch')
- d_prefix_keys: bfloat16 [64, 4, 512, 512], P('dp', 'branch')
- d_prefix_values: bfloat16 [64, 4, 512, 512], P('dp', 'branch')
- q_gain_grad: float32 [128], replicated
- k_gain_grad: float32 [128], replicated
The draws below stay inside these ranges and needn't reach their ends.
Inputs may be any that keep to these rules, and one draw needn't show every extreme that they name: `lengths`: every device has a slot whose length is exactly 32. `slot_prompt`: each prompt of a group is answered by exactly 8 slots of the group, none on the device that holds its prefix. `prefix_owner`: each row is a permutation of the group's devices.
All inputs are finite; a program needn't handle non-finite values.
Results may differ from the reference program's by a relative error of at most 0.014.
Values may be sent and summed in bfloat16 or wider, within the bound.
A program may use at most 128 MiB of HBM per device.

```python
import math
import jax
import jax.numpy as jnp
from jax import lax

HD = 128
KVH = 4
SLOTS = 8
PREFIX = 512
RMAX = 32
QW = 4096
KVW = 512
N_DP = 64
N_BRANCH = 4


def shared_owner(key):
    group_keys = jax.random.split(key, N_DP)
    return jax.vmap(lambda one_key: jax.random.permutation(one_key, N_BRANCH))(group_keys).astype(jnp.int32)


def draw_prefix_owner(key, part):
    return shared_owner(key)


def draw_slot_prompt(key, part):
    owner = shared_owner(key)
    key = jax.random.fold_in(key, 7)
    offset_key, order_key = jax.random.split(key)
    offset = jax.random.randint(offset_key, (N_DP, 1, 1), 0, N_BRANCH - 1)
    device = jnp.arange(N_BRANCH, dtype=jnp.int32)[None, :, None]
    slot_ids = jnp.arange(SLOTS, dtype=jnp.int32)[None, None, :]
    holder = (device + 1 + (slot_ids + offset) % (N_BRANCH - 1)) % N_BRANCH
    indices = jnp.arange(N_BRANCH, dtype=jnp.int32)
    matches = owner[:, None, :] == indices[None, :, None]
    inverse = jnp.sum(jnp.where(matches, indices[None, None, :], 0), axis=2).astype(jnp.int32)
    prompts = jnp.take_along_axis(inverse, holder.reshape(N_DP, -1), axis=1).reshape(N_DP, N_BRANCH, SLOTS)
    scores = jax.random.randint(order_key, (N_DP, N_BRANCH, SLOTS), 0, 1000) * SLOTS + slot_ids
    order = jnp.argsort(scores, axis=-1, stable=True)
    return jnp.take_along_axis(prompts, order, axis=-1).astype(jnp.int32)


def draw_lengths(key, part):
    key = jax.random.fold_in(key, 11)
    base_key, pick_key = jax.random.split(key)
    base = jax.random.randint(base_key, (N_DP, N_BRANCH, SLOTS), 1, RMAX + 1)
    pick = jax.random.randint(pick_key, (N_DP, N_BRANCH, 1), 0, SLOTS)
    slot_ids = jnp.arange(SLOTS, dtype=jnp.int32)[None, None, :]
    return jnp.where(slot_ids == pick, RMAX, base).astype(jnp.int32)


def shard_levels(own_key, extent, pieces, low, high):
    level, own = 1.0, jax.random.fold_in(own_key, 6)
    for position, shards_of in pieces:
        draws = jnp.exp(jax.random.uniform(jax.random.fold_in(own, position), (shards_of,), jnp.float32, low / len(pieces), high / len(pieces)))
        level = level * jnp.repeat(draws, extent[position] // shards_of).reshape([-1 if axis == position else 1 for axis in range(len(extent))])
    return level


def scatter_about(stream_key, dims, spread, bound, cuts=(), held_as=jnp.bfloat16):
    level = shard_levels(stream_key, dims, cuts, -0.22, 0.18) if cuts else 1.0
    values = jax.random.normal(stream_key, dims, jnp.float32) * spread * level
    return jnp.minimum(jnp.maximum(values, -bound), bound).astype(held_as)


def setup_inputs(seed: int = 0) -> dict:
    key_of = jax.random.split(jax.random.key(seed), 12)
    return {
        "prefix_keys": scatter_about(key_of[0], (N_DP, N_BRANCH, PREFIX, KVW), 1.0, 6.0, ((0, 64), (1, 4))),
        "prefix_values": scatter_about(key_of[1], (N_DP, N_BRANCH, PREFIX, KVW), 1.0, 6.0, ((0, 64), (1, 4))),
        "resp_query": scatter_about(key_of[2], (N_DP, N_BRANCH, SLOTS, RMAX, QW), 1.0, 6.0, ((0, 64), (1, 4))),
        "resp_keys": scatter_about(key_of[3], (N_DP, N_BRANCH, SLOTS, RMAX, KVW), 1.0, 6.0, ((0, 64), (1, 4))),
        "resp_values": scatter_about(key_of[4], (N_DP, N_BRANCH, SLOTS, RMAX, KVW), 1.0, 6.0, ((0, 64), (1, 4))),
        "out_grad": scatter_about(key_of[5], (N_DP, N_BRANCH, SLOTS, RMAX, QW), 1.0, 6.0, ((0, 64), (1, 4))),
        "q_gain": jnp.clip(1.0 + 0.18 * jax.random.normal(key_of[6], (HD,), jnp.float32), 0.1, 1.9),
        "k_gain": jnp.clip(1.0 + 0.18 * jax.random.normal(key_of[7], (HD,), jnp.float32), 0.1, 1.9),
        "lengths": draw_lengths(jax.random.fold_in(key_of[11], 71), 0),
        "slot_prompt": draw_slot_prompt(jax.random.fold_in(key_of[11], 71), 0),
        "prefix_owner": draw_prefix_owner(jax.random.fold_in(key_of[11], 71), 0),
    }


EPSILON = 1e-06

def product(pattern, first_op, second_op):
    return jnp.einsum(pattern, first_op.astype(jnp.float32), second_op.astype(jnp.float32))

def norm_forward(raw_vals, gain_vec):
    inv_rms = lax.rsqrt(lax.optimization_barrier(jnp.mean(raw_vals * raw_vals, axis=-1, keepdims=True)) + EPSILON)
    normed = raw_vals * inv_rms
    return ((normed * gain_vec).astype(jnp.bfloat16), normed, inv_rms)

def norm_backward(grad_hat, normed, inv_rms, gain_vec):
    scaled_grad = grad_hat * gain_vec
    grad_raw = inv_rms * (scaled_grad - normed * lax.optimization_barrier(jnp.mean(scaled_grad * normed, axis=-1, keepdims=True)))
    gain_grad = lax.optimization_barrier(jnp.sum(grad_hat * normed, axis=tuple(range(grad_hat.ndim - 1))))
    return (grad_raw, gain_grad)

def slot_pass(queries, resp_k, resp_v, grad_in, length, pre_k, pre_v, q_gain, k_gain):
    head_size = q_gain.shape[0]
    resp_len = queries.shape[0]
    q_heads = queries.shape[1] // head_size
    kv_heads = resp_k.shape[1] // head_size
    group_size = q_heads // kv_heads
    pre_len = pre_k.shape[0]
    q_hat, q_normed, q_inv = norm_forward(queries.astype(jnp.float32).reshape(resp_len, q_heads, head_size), q_gain)
    k_hat, k_normed, k_inv = norm_forward(resp_k.astype(jnp.float32).reshape(resp_len, kv_heads, head_size), k_gain)
    all_keys = jnp.concatenate([pre_k.reshape(pre_len, kv_heads, head_size), k_hat], axis=0)
    all_vals = jnp.concatenate([pre_v.reshape(pre_len, kv_heads, head_size), resp_v.reshape(resp_len, kv_heads, head_size)], axis=0)
    grouped_q = q_hat.reshape(resp_len, kv_heads, group_size, head_size)
    score_scale = 1.0 / math.sqrt(head_size)
    row_pos = jnp.arange(resp_len, dtype=jnp.int32)
    key_pos = jnp.arange(pre_len + resp_len, dtype=jnp.int32)
    allowed = (key_pos[None, :] < pre_len) | (key_pos[None, :] - pre_len <= row_pos[:, None])
    raw_scores = product('rhgd,jhd->hrgj', grouped_q, all_keys) * score_scale
    raw_scores = jnp.where(allowed[None, :, None, :], raw_scores, -1e+30)
    row_peak = lax.optimization_barrier(jnp.max(raw_scores, axis=-1, keepdims=True))
    shifted = jnp.exp(raw_scores - row_peak)
    attn_probs = shifted / lax.optimization_barrier(jnp.sum(shifted, axis=-1, keepdims=True))
    probs_low = attn_probs.astype(jnp.bfloat16)
    live_rows = row_pos < length
    mixed = product('hrgj,jhd->rhgd', probs_low, all_vals).reshape(resp_len, q_heads * head_size)
    attended = jnp.where(live_rows[:, None], mixed, 0.0).astype(jnp.bfloat16)
    grad_out = jnp.where(live_rows[:, None], grad_in, jnp.zeros_like(grad_in)).reshape(resp_len, kv_heads, group_size, head_size)
    grad_prob = product('rhgd,jhd->hrgj', grad_out, all_vals)
    row_total = lax.optimization_barrier(jnp.sum(attn_probs * grad_prob, axis=-1, keepdims=True))
    grad_score = (attn_probs * (grad_prob - row_total) * score_scale).astype(jnp.bfloat16)
    grad_q_hat = product('hrgj,jhd->rhgd', grad_score, all_keys).reshape(resp_len, q_heads, head_size)
    grad_keys = product('hrgj,rhgd->jhd', grad_score, grouped_q)
    grad_vals = product('hrgj,rhgd->jhd', probs_low, grad_out)
    grad_q, q_gain_part = norm_backward(grad_q_hat, q_normed, q_inv, q_gain)
    grad_k, k_gain_part = norm_backward(grad_keys[pre_len:], k_normed, k_inv, k_gain)
    return (attended, grad_q.reshape(resp_len, -1).astype(jnp.bfloat16), grad_k.reshape(resp_len, -1).astype(jnp.bfloat16), grad_vals[pre_len:].reshape(resp_len, -1).astype(jnp.bfloat16), grad_keys[:pre_len].reshape(pre_len, -1), grad_vals[:pre_len].reshape(pre_len, -1), q_gain_part, k_gain_part)

def device_pass(queries, resp_k, resp_v, grad_in, slot_lengths, owners, all_pre_k, all_pre_v, q_gain, k_gain):
    owner_count, pre_len, kv_width = all_pre_k.shape
    head_size = q_gain.shape[0]
    start = (jnp.zeros((owner_count, pre_len, kv_width), jnp.float32), jnp.zeros((owner_count, pre_len, kv_width), jnp.float32), jnp.zeros((head_size,), jnp.float32), jnp.zeros((head_size,), jnp.float32))

    def step(carry, inputs):
        slot_q, slot_k, slot_v, slot_g, length, owner = inputs
        pre_k = lax.dynamic_index_in_dim(all_pre_k, owner, 0, keepdims=False)
        pre_v = lax.dynamic_index_in_dim(all_pre_v, owner, 0, keepdims=False)
        results = slot_pass(slot_q, slot_k, slot_v, slot_g, length, pre_k, pre_v, q_gain, k_gain)
        acc_k, acc_v, q_acc, k_acc = carry
        acc_k = lax.dynamic_update_index_in_dim(acc_k, lax.dynamic_index_in_dim(acc_k, owner, 0, keepdims=False) + results[4], owner, 0)
        acc_v = lax.dynamic_update_index_in_dim(acc_v, lax.dynamic_index_in_dim(acc_v, owner, 0, keepdims=False) + results[5], owner, 0)
        return ((acc_k, acc_v, q_acc + results[6], k_acc + results[7]), results[:4])
    carry, stacked = lax.scan(step, start, (queries, resp_k, resp_v, grad_in, slot_lengths, owners))
    return (stacked, carry)

def reference(prefix_keys, prefix_values, resp_query, resp_keys, resp_values, out_grad, q_gain, k_gain, lengths, slot_prompt, prefix_owner):
    own_keys = prefix_keys.astype(jnp.float32).reshape(N_DP, N_BRANCH, PREFIX, KVH, HD)
    pre_hat, pre_normed, pre_inv = norm_forward(own_keys, k_gain)
    pre_hat = pre_hat.reshape(N_DP, N_BRANCH, PREFIX, KVW)
    start = (jnp.zeros((N_DP, N_BRANCH, PREFIX, KVW), jnp.float32), jnp.zeros((N_DP, N_BRANCH, PREFIX, KVW), jnp.float32), jnp.zeros((HD,), jnp.float32), jnp.zeros((HD,), jnp.float32))

    def per_device(carry, flat_index):
        group = flat_index // N_BRANCH
        member = flat_index % N_BRANCH
        owners = prefix_owner[group][slot_prompt[group, member]].astype(jnp.int32)
        stacked, sums = device_pass(resp_query[group, member], resp_keys[group, member], resp_values[group, member], out_grad[group, member], lengths[group, member], owners, pre_hat[group], prefix_values[group], q_gain, k_gain)
        low_k, low_v = lax.optimization_barrier((sums[0].astype(jnp.bfloat16), sums[1].astype(jnp.bfloat16)))
        acc_k, acc_v, q_acc, k_acc = carry
        acc_k = acc_k.at[group].add(low_k.astype(jnp.float32))
        acc_v = acc_v.at[group].add(low_v.astype(jnp.float32))
        return ((acc_k, acc_v, q_acc + sums[2], k_acc + sums[3]), stacked)
    carry, stacked = lax.scan(per_device, start, jnp.arange(N_DP * N_BRANCH, dtype=jnp.int32))
    acc_k, acc_v, q_total, k_total = carry
    attended = stacked[0].reshape(N_DP, N_BRANCH, SLOTS, RMAX, QW)
    d_query = stacked[1].reshape(N_DP, N_BRANCH, SLOTS, RMAX, QW)
    d_resp_keys = stacked[2].reshape(N_DP, N_BRANCH, SLOTS, RMAX, KVW)
    d_resp_values = stacked[3].reshape(N_DP, N_BRANCH, SLOTS, RMAX, KVW)
    grad_pre, pre_gain = norm_backward(acc_k.reshape(N_DP, N_BRANCH, PREFIX, KVH, HD), pre_normed, pre_inv, k_gain)
    d_prefix_keys = grad_pre.reshape(N_DP, N_BRANCH, PREFIX, KVW).astype(jnp.bfloat16)
    d_prefix_values = acc_v.astype(jnp.bfloat16)
    return (attended, d_query, d_resp_keys, d_resp_values, d_prefix_keys, d_prefix_values, q_total, k_total + pre_gain)
```

```python
import functools
import math

import jax
import jax.numpy as jnp
from jax import lax
from jax.experimental import pallas as pl
from jax.experimental.pallas import tpu as pltpu
from jax.sharding import PartitionSpec as P

EPSILON = 1e-06
MESH = pl.DeviceIdType.MESH
F32 = jnp.float32
BF16 = jnp.bfloat16
LOG2E = math.log2(math.e)
LN2 = math.log(2.0)


def dot(a, b):
    return lax.dot_general(a, b, (((1,), (0,)), ((), ())), preferred_element_type=F32)


def dot_nt(a, b):
    return lax.dot_general(a, b, (((1,), (1,)), ((), ())), preferred_element_type=F32)


def norm_parts(raw):
    vals = raw.astype(F32)
    inv = lax.rsqrt(jnp.mean(vals * vals, axis=-1, keepdims=True) + EPSILON)
    return vals * inv, inv


def kernel(
    dims,
    pk, pv, q, rk, rv, g, q_gain, k_gain, lengths, prompts, owners,
    att, dq, d_rk, d_rv, d_pk, d_pv, qg_out, kg_out,
    qv, gv, attv, dqv, rkv, rvv, drkv, drvv, kraw,
    kb0, kb1, kb2, kb3, vb0, vb1, vb2, vb3,
    kt, vt, ck, cv, es, eb, ub, gq, gacc, rs_out, rs_in, dpk, dpv, ex1, ex2, ex3, meta,
    ag_send, ag_recv, rs_send, rs_recv, gx_send, gx_recv, load_sem, store_sem,
):
    n_dp, n_branch, inner, slots, rows, heads, group, pre, hd = dims
    outer = n_dp // inner
    kb, vb = (kb0, kb1, kb2, kb3), (vb0, vb1, vb2, vb3)
    width = group * hd
    cols = group * rows
    score_scale = 1.0 / math.sqrt(hd)

    me = lax.axis_index("branch")
    dp = lax.axis_index("dp")
    right = lax.rem(me + 1, n_branch)
    left = lax.rem(me + n_branch - 1, n_branch)
    in_c = lax.rem(dp, inner)
    out_c = dp // inner
    stages = (
        (ex1, me, n_branch, lambda k: {"branch": lax.rem(me + k, n_branch)}),
        (ex2, in_c, inner, lambda k: {"dp": out_c * inner + lax.rem(in_c + k, inner)}),
        (ex3, out_c, outer, lambda k: {"dp": lax.rem(out_c + k, outer) * inner + in_c}),
    )

    def head_cols(h):
        return pl.ds(h * hd, hd)

    k_loads = [
        pltpu.make_async_copy(pk.at[:, head_cols(h)], kraw.at[h], load_sem.at[h])
        for h in range(heads)
    ]
    v_loads = [
        pltpu.make_async_copy(pv.at[:, head_cols(h)], vb[h].at[0], load_sem.at[heads + h])
        for h in range(heads)
    ]
    base = 2 * heads
    rest_loads = [
        pltpu.make_async_copy(src, dst, load_sem.at[base + i])
        for i, (src, dst) in enumerate(((q, qv), (g, gv), (rk, rkv), (rv, rvv)))
    ]
    for h in range(heads):
        k_loads[h].start()
        v_loads[h].start()
    for copy in rest_loads:
        copy.start()

    barrier = pltpu.get_barrier_semaphore()
    partners = 0
    for _, _, extent, partner in stages:
        for k in range(1, extent):
            pl.semaphore_signal(barrier, inc=1, device_id=partner(k), device_id_type=MESH)
            partners += 1

    kg_row = k_gain[...]
    qg_row = q_gain[...]

    def own_hat(h):
        k_loads[h].wait()
        normed, _ = norm_parts(kraw[h])
        kb[h][0] = (normed * kg_row).astype(BF16)
        v_loads[h].wait()

    def remote(src, dst, send, recv, to):
        return pltpu.make_async_remote_copy(
            src_ref=src, dst_ref=dst, send_sem=send, recv_sem=recv,
            device_id={"branch": to}, device_id_type=MESH,
        )

    def ag(h, i):
        src, dst, to = (
            (kb[h].at[0], kb[h].at[3], right),
            (vb[h].at[0], vb[h].at[1], left),
            (vb[h].at[0], vb[h].at[3], right),
            (kb[h].at[0], kb[h].at[1], left),
            (kb[h].at[3], kb[h].at[2], right),
            (vb[h].at[1], vb[h].at[2], left),
        )[i]
        return remote(src, dst, ag_send.at[h, i], ag_recv.at[h, i], to)

    def ag_direct(h):
        for i in range(4):
            ag(h, i).start()

    def ag_forward(h):
        ag(h, 0).wait_recv()
        ag(h, 4).start()
        ag(h, 1).wait_recv()
        ag(h, 5).start()

    def ag_rest(h):
        for i in range(2, 6):
            ag(h, i).wait_recv()

    def rs(h, i):
        to = right if i % 2 == 0 else left
        return remote(rs_out.at[h, i], rs_in.at[h, i], rs_send.at[h, i], rs_recv.at[h, i], to)

    def rs_first(h):
        def part(acc, scale, r):
            return acc[meta[2, r]] * scale

        rs_out[h, 0] = part(ck, LN2, 2).astype(BF16)
        rs(h, 0).start()
        rs_out[h, 1] = part(cv, 1.0, 2).astype(BF16)
        rs(h, 1).start()
        rs_out[h, 2] = part(cv, 1.0, 1).astype(BF16)
        rs(h, 2).start()
        rs_out[h, 3] = part(ck, LN2, 3).astype(BF16)
        rs(h, 3).start()
        rs_out[h, 4] = part(ck, LN2, 1).astype(BF16)
        rs_out[h, 5] = part(cv, 1.0, 3).astype(BF16)

    def rs_second(h):
        for i in (0, 1):
            rs(h, i).wait_recv()
            rs_out[h, 4 + i] = (rs_out[h, 4 + i].astype(F32) + rs_in[h, i].astype(F32)).astype(BF16)
            rs(h, 4 + i).start()

    def out_copy(src, dst, i):
        return pltpu.make_async_copy(src, dst, store_sem.at[i])

    def prefix_out(h):
        return (
            out_copy(dpk.at[h], d_pk.at[:, head_cols(h)], 2 * heads + h),
            out_copy(dpv.at[h], d_pv.at[:, head_cols(h)], 3 * heads + h),
        )

    def rs_final(h):
        for i in range(2, 6):
            rs(h, i).wait_recv()
        grad = rs_in[h, 3].astype(F32) + rs_in[h, 4].astype(F32)
        normed, inv = norm_parts(kraw[h])
        scaled = grad * kg_row
        back = inv * (scaled - normed * jnp.mean(scaled * normed, axis=-1, keepdims=True))
        dpk[h] = back.astype(BF16)
        dpv[h] = (rs_in[h, 2].astype(F32) + rs_in[h, 5].astype(F32)).astype(BF16)
        for copy in prefix_out(h):
            copy.start()

    def head_out(h):
        part = pl.ds(h * width, width)
        return (
            out_copy(attv.at[:, :, part], att.at[:, :, part], h),
            out_copy(dqv.at[:, :, part], dq.at[:, :, part], heads + h),
        )

    def transposes(h):
        for r in range(1, n_branch):
            kt[r] = kb[h][r].T
            vt[r] = vb[h][r].T

    block = 128
    lane = lax.broadcasted_iota(jnp.int32, (1, cols), 1)
    token = lane & (rows - 1)

    def slot_pass(s, h, u):
        rel = meta[0, s]
        prev = meta[1, s]
        live = token < lengths[s]
        at = [h * width + i * hd for i in range(group)]
        q_t = jnp.concatenate([qv[s, :, a : a + hd] for a in at], axis=0).T.astype(F32)
        g_t = jnp.concatenate([gv[s, :, a : a + hd] for a in at], axis=0).T.astype(F32)
        g_t = jnp.where(live, g_t, 0.0)
        g_low = g_t.astype(BF16)
        q_inv = lax.rsqrt(jnp.mean(q_t * q_t, axis=0, keepdims=True) + EPSILON)
        q_n = q_t * q_inv
        gain = gq[...]
        q_scaled = q_n * (gain * (LOG2E * score_scale))
        q_low = q_scaled.astype(BF16)
        k_n, k_inv = norm_parts(rkv[s, :, h * hd : (h + 1) * hd])
        k_low = (k_n * kg_row).astype(BF16)
        v_low = rvv[s, :, h * hd : (h + 1) * hd]

        allowed = lax.broadcasted_iota(jnp.int32, (rows, cols), 0) <= token
        e_r = jnp.where(allowed, jnp.exp2(dot(k_low, q_low)), 0.0)
        total = jnp.sum(e_r, axis=0, keepdims=True)
        for c in range(pre // block):
            part = pl.ds(c * block, block)
            e_c = jnp.exp2(dot(kb[h][rel, part, :], q_low))
            es[u, part, :] = e_c
            eb[u, part, :] = e_c.astype(BF16)
            total += jnp.sum(e_c, axis=0, keepdims=True)
        inv = 1.0 / total
        e_r_low = e_r.astype(BF16)
        o_t = (dot(vt[rel], eb[u]) + dot(v_low.T, e_r_low)) * inv
        dots = jnp.sum(g_t * o_t, axis=0, keepdims=True)
        o_low = jnp.where(live, o_t, 0.0).astype(BF16).T
        for i, a in enumerate(at):
            attv[s, :, a : a + hd] = o_low[i * rows : (i + 1) * rows, :]

        u_r = (e_r * (dot(v_low, g_low) - dots)).astype(BF16)
        for c in range(pre // block):
            part = pl.ds(c * block, block)
            d_c = dot(vb[h][rel, part, :], g_low)
            ub[u, part, :] = (es[u, part, :] * (d_c - dots)).astype(BF16)
        dq_t = (dot(kt[rel], ub[u]) + dot(k_low.T, u_r)) * (inv * score_scale)
        gacc[...] += q_n * dq_t
        scaled = gain * dq_t
        back = q_inv * (scaled - q_n * jnp.mean(scaled * q_n, axis=0, keepdims=True))
        back_low = back.astype(BF16).T
        for i, a in enumerate(at):
            dqv[s, :, a : a + hd] = back_low[i * rows : (i + 1) * rows, :]

        q_part = (q_scaled * inv).astype(BF16)
        g_part = (g_t * inv).astype(BF16)
        dk_r = dot_nt(u_r, q_part) * LN2
        scaled_k = dk_r * kg_row
        back_k = k_inv * (scaled_k - k_n * jnp.mean(scaled_k * k_n, axis=-1, keepdims=True))
        drkv[s, :, h * hd : (h + 1) * hd] = back_k.astype(BF16)
        drvv[s, :, h * hd : (h + 1) * hd] = dot_nt(e_r_low, g_part).astype(BF16)
        for c in range(pre // block):
            part = pl.ds(c * block, block)
            ck[s, part, :] = ck[prev, part, :] + dot_nt(ub[u, part, :], q_part)
            cv[s, part, :] = cv[prev, part, :] + dot_nt(eb[u, part, :], g_part)

    def run_slots(h, first, count):
        def step(i, carry):
            for u in range(2):
                slot_pass(first + 2 * i + u, h, u)
            return carry

        lax.fori_loop(0, count // 2, step, 0)

    own_hat(0)
    pl.semaphore_wait(barrier, partners)
    ag_direct(0)
    own_hat(1)
    ag_forward(0)
    ag_direct(1)
    for h in range(2, heads):
        own_hat(h)

    rels = []
    for s in range(slots):
        rel = owners[prompts[s]] - me
        rel = jnp.where(rel < 0, rel + n_branch, rel)
        prev = jnp.int32(slots)
        for before in range(s):
            prev = jnp.where(rels[before] == rel, before, prev)
        rels.append(rel)
        meta[0, s] = rel
        meta[1, s] = prev
    for r in range(1, n_branch):
        last = jnp.int32(slots)
        for s in range(slots):
            last = jnp.where(rels[s] == r, s, last)
        meta[2, r] = last
    ck[slots] = jnp.zeros((pre, hd), F32)
    cv[slots] = jnp.zeros((pre, hd), F32)
    gq[...] = jnp.broadcast_to(qg_row, (cols, hd)).T
    gacc[...] = jnp.zeros_like(gacc)
    for copy in rest_loads:
        copy.wait()

    half = slots // 2
    for h in range(heads):
        ag_rest(h)
        transposes(h)
        run_slots(h, 0, half)
        if h + 1 < heads:
            ag_forward(h + 1)
        if h + 2 < heads:
            ag_direct(h + 2)
        if h >= 2:
            rs_second(h - 2)
        run_slots(h, half, slots - half)
        rs_first(h)
        for copy in head_out(h):
            copy.start()
        if h >= 3:
            rs_final(h - 3)
    resp_out = (out_copy(drkv, d_rk, 4 * heads), out_copy(drvv, d_rv, 4 * heads + 1))
    for copy in resp_out:
        copy.start()

    value = jnp.sum(gacc[...].T, axis=0, keepdims=True)

    def exchange(i, value):
        buf, place, extent, partner = stages[i]
        buf[place] = jnp.broadcast_to(value, (8, hd))
        for k in range(1, extent):
            gain_copy(i, k).start()

    def gain_copy(i, k):
        buf, place, _, partner = stages[i]
        return pltpu.make_async_remote_copy(
            src_ref=buf.at[place], dst_ref=buf.at[place],
            send_sem=gx_send.at[i, k], recv_sem=gx_recv.at[i, k],
            device_id=partner(k), device_id_type=MESH,
        )

    def collect(i):
        buf, _, extent, _ = stages[i]
        for k in range(1, extent):
            gain_copy(i, k).wait_recv()
        value = buf[0]
        for k in range(1, extent):
            value = value + buf[k]
        return value[0:1, :]

    exchange(0, value)
    rs_second(heads - 2)
    exchange(1, collect(0))
    rs_second(heads - 1)
    rs_final(heads - 3)
    exchange(2, collect(1))
    rs_final(heads - 2)
    value = collect(2)
    qg_out[...] = value
    kg_out[...] = value * qg_row / kg_row
    rs_final(heads - 1)

    for h in range(heads):
        for i in range(6):
            ag(h, i).wait_send()
            rs(h, i).wait_send()
    for i, (_, _, extent, _) in enumerate(stages):
        for k in range(1, extent):
            gain_copy(i, k).wait_send()
    for h in range(heads):
        for copy in head_out(h) + prefix_out(h):
            copy.wait()
    for copy in resp_out:
        copy.wait()


def body(
    n_dp, n_branch,
    prefix_keys, prefix_values, resp_query, resp_keys, resp_values, out_grad,
    q_gain, k_gain, lengths, slot_prompt, prefix_owner,
):
    hd = q_gain.shape[0]
    pre, kvw = prefix_keys.shape[2:]
    slots, rows, qw = resp_query.shape[2:]
    heads = kvw // hd
    group = qw // kvw
    inner = math.gcd(n_dp, 8)
    outer = n_dp // inner
    cols = group * rows
    hbm = pl.BlockSpec(memory_space=pl.ANY)
    vmem = pl.BlockSpec(memory_space=pltpu.VMEM)
    smem = pl.BlockSpec(memory_space=pltpu.SMEM)

    def held(dtype, *shape):
        return pltpu.VMEM(shape, dtype)

    prefix_slots = [held(BF16, n_branch, pre, hd) for _ in range(2 * heads)]
    outs = pl.pallas_call(
        functools.partial(kernel, (n_dp, n_branch, inner, slots, rows, heads, group, pre, hd)),
        out_shape=(
            jax.ShapeDtypeStruct((slots, rows, qw), BF16),
            jax.ShapeDtypeStruct((slots, rows, qw), BF16),
            jax.ShapeDtypeStruct((slots, rows, kvw), BF16),
            jax.ShapeDtypeStruct((slots, rows, kvw), BF16),
            jax.ShapeDtypeStruct((pre, kvw), BF16),
            jax.ShapeDtypeStruct((pre, kvw), BF16),
            jax.ShapeDtypeStruct((1, hd), F32),
            jax.ShapeDtypeStruct((1, hd), F32),
        ),
        in_specs=[hbm] * 6 + [vmem] * 2 + [smem] * 3,
        out_specs=(hbm,) * 6 + (vmem,) * 2,
        scratch_shapes=[
            held(BF16, slots, rows, qw),
            held(BF16, slots, rows, qw),
            held(BF16, slots, rows, qw),
            held(BF16, slots, rows, qw),
            held(BF16, slots, rows, kvw),
            held(BF16, slots, rows, kvw),
            held(BF16, slots, rows, kvw),
            held(BF16, slots, rows, kvw),
            held(BF16, heads, pre, hd),
            *prefix_slots,
            held(BF16, n_branch, hd, pre),
            held(BF16, n_branch, hd, pre),
            held(F32, slots + 1, pre, hd),
            held(F32, slots + 1, pre, hd),
            held(F32, 2, pre, cols),
            held(BF16, 2, pre, cols),
            held(BF16, 2, pre, cols),
            held(F32, hd, cols),
            held(F32, hd, cols),
            held(BF16, heads, 6, pre, hd),
            held(BF16, heads, 6, pre, hd),
            held(BF16, heads, pre, hd),
            held(BF16, heads, pre, hd),
            held(F32, n_branch, 8, hd),
            held(F32, inner, 8, hd),
            held(F32, outer, 8, hd),
            pltpu.SMEM((3, slots), jnp.int32),
            pltpu.SemaphoreType.DMA((heads, 6)),
            pltpu.SemaphoreType.DMA((heads, 6)),
            pltpu.SemaphoreType.DMA((heads, 6)),
            pltpu.SemaphoreType.DMA((heads, 6)),
            pltpu.SemaphoreType.DMA((3, 8)),
            pltpu.SemaphoreType.DMA((3, 8)),
            pltpu.SemaphoreType.DMA((2 * heads + 4,)),
            pltpu.SemaphoreType.DMA((4 * heads + 2,)),
        ],
        compiler_params=pltpu.CompilerParams(
            collective_id=0, has_side_effects=True, vmem_limit_bytes=56 * 1024 * 1024
        ),
    )(
        prefix_keys[0, 0], prefix_values[0, 0], resp_query[0, 0], resp_keys[0, 0],
        resp_values[0, 0], out_grad[0, 0], q_gain[None], k_gain[None],
        lengths[0, 0], slot_prompt[0, 0], prefix_owner[0],
    )
    return tuple(x[None, None] for x in outs[:6]) + (outs[6][0], outs[7][0])


def solution(mesh):
    block = P("dp", "branch")
    return jax.shard_map(
        functools.partial(body, mesh.shape["dp"], mesh.shape["branch"]),
        mesh=mesh,
        in_specs=(block,) * 6 + (P(), P()) + (block, block, P("dp")),
        out_specs=(block,) * 6 + (P(), P()),
        check_vma=False,
    )
```

```python
import functools
import math

import jax
import jax.numpy as jnp
from jax import lax
from jax.experimental import pallas as pl
from jax.experimental.pallas import tpu as pltpu
from jax.sharding import PartitionSpec as P

EPSILON = 1e-06
MESH = pl.DeviceIdType.MESH
F32 = jnp.float32
BF16 = jnp.bfloat16
LOG2E = math.log2(math.e)
LN2 = math.log(2.0)


def dot(a, b):
    return lax.dot_general(a, b, (((1,), (0,)), ((), ())), preferred_element_type=F32)


def dot_nt(a, b):
    return lax.dot_general(a, b, (((1,), (1,)), ((), ())), preferred_element_type=F32)


def norm_parts(raw):
    vals = raw.astype(F32)
    inv = lax.rsqrt(jnp.mean(vals * vals, axis=-1, keepdims=True) + EPSILON)
    return vals * inv, inv


def kernel(
    dims,
    pk, pv, q, rk, rv, g, q_gain, k_gain, lengths, prompts, owners,
    attv, dqv, drkv, drvv, dpk, dpv, qg_out, kg_out,
    qv, gv, rkv, rvv, kraw,
    kb0, kb1, kb2, kb3, vb0, vb1, vb2, vb3,
    kt, vt, ck, cv, es, eb, ub, gq, gacc, rs_out, rs_in, ex1, ex2, ex3, ex4, meta,
    ag_send, ag_recv, rs_send, rs_recv, gx_send, gx_recv, load_sem, ready,
):
    n_dp, n_branch, inner, slots, rows, heads, group, pre, hd = dims
    outer = n_dp // inner
    kb, vb = (kb0, kb1, kb2, kb3), (vb0, vb1, vb2, vb3)
    width = group * hd
    cols = group * rows
    score_scale = 1.0 / math.sqrt(hd)

    me = lax.axis_index("branch")
    dp = lax.axis_index("dp")
    right = lax.rem(me + 1, n_branch)
    left = lax.rem(me + n_branch - 1, n_branch)
    in_c = lax.rem(dp, inner)
    out_c = dp // inner
    stages = (
        (ex2, in_c, inner, lambda k: {"dp": out_c * inner + lax.rem(in_c + k, inner)}),
        (ex3, out_c, outer, lambda k: {"dp": lax.rem(out_c + k, outer) * inner + in_c}),
    )
    met = inner + outer - 2

    barrier = pltpu.get_barrier_semaphore()

    def tell(sem, to):
        pl.semaphore_signal(sem, inc=1, device_id=to, device_id_type=MESH)

    @pl.when(me == 2)
    def _():
        tell(barrier, {"branch": 1})
        tell(barrier, {"branch": 3})

    @pl.when((me == 1) | (me == 3))
    def _():
        tell(barrier, {"branch": 2})

    @pl.when(me == 0)
    def _():
        for k in (1, 3, 2):
            tell(barrier, {"branch": k})
        for _, _, extent, partner in stages:
            for k in range(1, extent):
                tell(barrier, partner(k))

    def enter():
        @pl.when(me == 2)
        def _():
            pl.semaphore_wait(barrier, 3)
            tell(ready.at[1], {"branch": 0})

        @pl.when((me == 1) | (me == 3))
        def _():
            pl.semaphore_wait(barrier, 2)
            tell(ready.at[0], {"branch": 0})

        @pl.when(me == 0)
        def _():
            pl.semaphore_wait(ready.at[0], 2)

    def head_cols(h):
        return pl.ds(h * hd, hd)

    k_loads = [
        pltpu.make_async_copy(pk.at[:, head_cols(h)], kraw.at[h], load_sem.at[h])
        for h in range(heads)
    ]
    v_loads = [
        pltpu.make_async_copy(pv.at[:, head_cols(h)], vb[h].at[0], load_sem.at[heads + h])
        for h in range(heads)
    ]
    base = 2 * heads
    rest_loads = [
        pltpu.make_async_copy(src, dst, load_sem.at[base + i])
        for i, (src, dst) in enumerate(((q, qv), (g, gv), (rk, rkv), (rv, rvv)))
    ]
    for h in range(heads):
        k_loads[h].start()
        v_loads[h].start()
    for copy in rest_loads:
        copy.start()

    kg_row = k_gain[...]
    qg_row = q_gain[...]

    def own_hat(h):
        k_loads[h].wait()
        normed, _ = norm_parts(kraw[h])
        kb[h][0] = (normed * kg_row).astype(BF16)
        v_loads[h].wait()

    def remote(src, dst, send, recv, to):
        return pltpu.make_async_remote_copy(
            src_ref=src, dst_ref=dst, send_sem=send, recv_sem=recv,
            device_id={"branch": to}, device_id_type=MESH,
        )

    def ag(h, i):
        src, dst, to = (
            (kb[h].at[0], kb[h].at[3], right),
            (vb[h].at[0], vb[h].at[1], left),
            (vb[h].at[0], vb[h].at[3], right),
            (kb[h].at[0], kb[h].at[1], left),
            (kb[h].at[3], kb[h].at[2], right),
            (vb[h].at[1], vb[h].at[2], left),
        )[i]
        return remote(src, dst, ag_send.at[h, i], ag_recv.at[h, i], to)

    def ag_direct(h):
        for i in range(4):
            ag(h, i).start()

    def ag_forward(h):
        ag(h, 0).wait_recv()
        ag(h, 4).start()
        ag(h, 1).wait_recv()
        ag(h, 5).start()

    def ag_rest(h):
        for i in range(2, 6):
            ag(h, i).wait_recv()

    def rs(h, i):
        to = right if i % 2 == 0 else left
        return remote(rs_out.at[h, i], rs_in.at[h, i], rs_send.at[h, i], rs_recv.at[h, i], to)

    def rs_first(h):
        def part(acc, scale, r):
            return acc[meta[2, r]] * scale

        rs_out[h, 0] = part(ck, LN2, 2).astype(BF16)
        rs(h, 0).start()
        rs_out[h, 1] = part(cv, 1.0, 2).astype(BF16)
        rs(h, 1).start()
        rs_out[h, 2] = part(cv, 1.0, 1).astype(BF16)
        rs(h, 2).start()
        rs_out[h, 3] = part(ck, LN2, 3).astype(BF16)
        rs(h, 3).start()
        rs_out[h, 4] = part(ck, LN2, 1).astype(BF16)
        rs_out[h, 5] = part(cv, 1.0, 3).astype(BF16)

    def rs_second(h):
        for i in (0, 1):
            rs(h, i).wait_recv()
            rs_out[h, 4 + i] = (rs_out[h, 4 + i].astype(F32) + rs_in[h, i].astype(F32)).astype(BF16)
            rs(h, 4 + i).start()

    def rs_final(h):
        for i in range(2, 6):
            rs(h, i).wait_recv()
        grad = rs_in[h, 3].astype(F32) + rs_in[h, 4].astype(F32)
        normed, inv = norm_parts(kraw[h])
        scaled = grad * kg_row
        back = inv * (scaled - normed * jnp.mean(scaled * normed, axis=-1, keepdims=True))
        dpk[:, h * hd : (h + 1) * hd] = back.astype(BF16)
        dpv[:, h * hd : (h + 1) * hd] = (rs_in[h, 2].astype(F32) + rs_in[h, 5].astype(F32)).astype(BF16)

    def transposes(h):
        for r in range(1, n_branch):
            kt[r] = kb[h][r].T
            vt[r] = vb[h][r].T

    block = 128
    lane = lax.broadcasted_iota(jnp.int32, (1, cols), 1)
    token = lane & (rows - 1)

    def slot_pass(s, h, u):
        rel = meta[0, s]
        prev = meta[1, s]
        live = token < lengths[s]
        at = [h * width + i * hd for i in range(group)]
        q_t = jnp.concatenate([qv[s, :, a : a + hd] for a in at], axis=0).T.astype(F32)
        g_t = jnp.concatenate([gv[s, :, a : a + hd] for a in at], axis=0).T.astype(F32)
        g_t = jnp.where(live, g_t, 0.0)
        g_low = g_t.astype(BF16)
        q_inv = lax.rsqrt(jnp.mean(q_t * q_t, axis=0, keepdims=True) + EPSILON)
        q_n = q_t * q_inv
        gain = gq[...]
        q_scaled = q_n * (gain * (LOG2E * score_scale))
        q_low = q_scaled.astype(BF16)
        k_n, k_inv = norm_parts(rkv[s, :, h * hd : (h + 1) * hd])
        k_low = (k_n * kg_row).astype(BF16)
        v_low = rvv[s, :, h * hd : (h + 1) * hd]

        allowed = lax.broadcasted_iota(jnp.int32, (rows, cols), 0) <= token
        e_r = jnp.where(allowed, jnp.exp2(dot(k_low, q_low)), 0.0)
        total = jnp.sum(e_r, axis=0, keepdims=True)
        for c in range(pre // block):
            part = pl.ds(c * block, block)
            e_c = jnp.exp2(dot(kb[h][rel, part, :], q_low))
            es[u, part, :] = e_c
            eb[u, part, :] = e_c.astype(BF16)
            total += jnp.sum(e_c, axis=0, keepdims=True)
        inv = 1.0 / total
        e_r_low = e_r.astype(BF16)
        o_t = (dot(vt[rel], eb[u]) + dot(v_low.T, e_r_low)) * inv
        dots = jnp.sum(g_t * o_t, axis=0, keepdims=True)
        o_low = jnp.where(live, o_t, 0.0).astype(BF16).T
        for i, a in enumerate(at):
            attv[s, :, a : a + hd] = o_low[i * rows : (i + 1) * rows, :]

        u_r = (e_r * (dot(v_low, g_low) - dots)).astype(BF16)
        for c in range(pre // block):
            part = pl.ds(c * block, block)
            d_c = dot(vb[h][rel, part, :], g_low)
            ub[u, part, :] = (es[u, part, :] * (d_c - dots)).astype(BF16)
        dq_t = (dot(kt[rel], ub[u]) + dot(k_low.T, u_r)) * (inv * score_scale)
        gacc[...] += q_n * dq_t
        scaled = gain * dq_t
        back = q_inv * (scaled - q_n * jnp.mean(scaled * q_n, axis=0, keepdims=True))
        back_low = back.astype(BF16).T
        for i, a in enumerate(at):
            dqv[s, :, a : a + hd] = back_low[i * rows : (i + 1) * rows, :]

        q_part = (q_scaled * inv).astype(BF16)
        g_part = (g_t * inv).astype(BF16)
        dk_r = dot_nt(u_r, q_part) * LN2
        scaled_k = dk_r * kg_row
        back_k = k_inv * (scaled_k - k_n * jnp.mean(scaled_k * k_n, axis=-1, keepdims=True))
        drkv[s, :, h * hd : (h + 1) * hd] = back_k.astype(BF16)
        drvv[s, :, h * hd : (h + 1) * hd] = dot_nt(e_r_low, g_part).astype(BF16)
        for c in range(pre // block):
            part = pl.ds(c * block, block)
            ck[s, part, :] = ck[prev, part, :] + dot_nt(ub[u, part, :], q_part)
            cv[s, part, :] = cv[prev, part, :] + dot_nt(eb[u, part, :], g_part)

    def run_slots(h, first, count):
        def step(i, carry):
            for u in range(2):
                slot_pass(first + 2 * i + u, h, u)
            return carry

        lax.fori_loop(0, count // 2, step, 0)

    own_hat(0)
    enter()
    ag_direct(0)
    own_hat(1)
    ag_forward(0)
    ag_direct(1)
    for h in range(2, heads):
        own_hat(h)

    rels = []
    for s in range(slots):
        rel = owners[prompts[s]] - me
        rel = jnp.where(rel < 0, rel + n_branch, rel)
        prev = jnp.int32(slots)
        for before in range(s):
            prev = jnp.where(rels[before] == rel, before, prev)
        rels.append(rel)
        meta[0, s] = rel
        meta[1, s] = prev
    for r in range(1, n_branch):
        last = jnp.int32(slots)
        for s in range(slots):
            last = jnp.where(rels[s] == r, s, last)
        meta[2, r] = last
    ck[slots] = jnp.zeros((pre, hd), F32)
    cv[slots] = jnp.zeros((pre, hd), F32)
    gq[...] = jnp.broadcast_to(qg_row, (cols, hd)).T
    gacc[...] = jnp.zeros_like(gacc)
    for copy in rest_loads:
        copy.wait()

    half = slots // 2
    for h in range(heads):
        ag_rest(h)
        transposes(h)
        run_slots(h, 0, half)
        if h + 1 < heads:
            ag_forward(h + 1)
        if h + 2 < heads:
            ag_direct(h + 2)
        if h >= 2:
            rs_second(h - 2)
        run_slots(h, half, slots - half)
        if h + 1 < heads:
            rs_first(h)
        if h >= 3:
            rs_final(h - 3)

    def spread(value):
        return jnp.broadcast_to(value, (8, hd))

    ex1[me] = spread(jnp.sum(gacc[...].T, axis=0, keepdims=True))

    def gain_copy(src, dst, i, k, j, to):
        return pltpu.make_async_remote_copy(
            src_ref=src, dst_ref=dst, send_sem=gx_send.at[i, k], recv_sem=gx_recv.at[i, j],
            device_id=to, device_id_type=MESH,
        )

    def up(place):
        return gain_copy(ex1.at[place], ex1.at[place], 0, 0, place, {"branch": 0})

    def down(k):
        return gain_copy(ex4, ex4, 3, k, 0, {"branch": k})

    def across(i, k):
        buf, place, _, partner = stages[i]
        return gain_copy(buf.at[place], buf.at[place], 1 + i, k, k, partner(k))

    def collect(buf, extent, copies):
        for copy in copies:
            copy.wait_recv()
        value = buf[0]
        for k in range(1, extent):
            value = value + buf[k]
        return value

    def send_across(i, value):
        buf, place, extent, _ = stages[i]
        buf[place] = value
        for k in range(1, extent):
            across(i, k).start()

    def collect_across(i):
        buf, _, extent, _ = stages[i]
        return collect(buf, extent, [across(i, k) for k in range(1, extent)])

    @pl.when(me != 0)
    def _():
        up(me).start()

    rs_first(heads - 1)
    rs_second(heads - 2)

    @pl.when(me == 0)
    def _():
        value = collect(ex1, n_branch, [up(k) for k in range(1, n_branch)])
        pl.semaphore_wait(barrier, met)
        send_across(0, value)

    rs_second(heads - 1)
    rs_final(heads - 3)

    @pl.when(me == 0)
    def _():
        send_across(1, collect_across(0))

    rs_final(heads - 2)

    @pl.when(me == 0)
    def _():
        ex4[...] = collect_across(1)
        pl.semaphore_wait(ready.at[1], 1)
        for k in range(1, n_branch):
            down(k).start()

    rs_final(heads - 1)

    @pl.when(me != 0)
    def _():
        down(me).wait_recv()

    value = ex4[0:1, :]
    qg_out[...] = value
    kg_out[...] = value * qg_row / kg_row

    for h in range(heads):
        for i in range(6):
            ag(h, i).wait_send()
            rs(h, i).wait_send()

    @pl.when(me != 0)
    def _():
        up(me).wait_send()

    @pl.when(me == 0)
    def _():
        for i, (_, _, extent, _) in enumerate(stages):
            for k in range(1, extent):
                across(i, k).wait_send()
        for k in range(1, n_branch):
            down(k).wait_send()


def write_out(*refs):
    count = len(refs) // 2
    held, outs, sems = refs[:count], refs[count:-1], refs[-1]
    copies = [pltpu.make_async_copy(a, b, sems.at[i]) for i, (a, b) in enumerate(zip(held, outs))]
    for copy in copies:
        copy.start()
    for copy in copies:
        copy.wait()


def body(
    n_dp, n_branch,
    prefix_keys, prefix_values, resp_query, resp_keys, resp_values, out_grad,
    q_gain, k_gain, lengths, slot_prompt, prefix_owner,
):
    hd = q_gain.shape[0]
    pre, kvw = prefix_keys.shape[2:]
    slots, rows, qw = resp_query.shape[2:]
    heads = kvw // hd
    group = qw // kvw
    inner = math.gcd(n_dp, 8)
    outer = n_dp // inner
    cols = group * rows
    hbm = pl.BlockSpec(memory_space=pltpu.HBM)
    vmem = pl.BlockSpec(memory_space=pltpu.VMEM)
    smem = pl.BlockSpec(memory_space=pltpu.SMEM)

    def held(dtype, *shape):
        return pltpu.VMEM(shape, dtype)

    prefix_slots = [held(BF16, n_branch, pre, hd) for _ in range(2 * heads)]
    shapes = (
        ((slots, rows, qw), BF16),
        ((slots, rows, qw), BF16),
        ((slots, rows, kvw), BF16),
        ((slots, rows, kvw), BF16),
        ((pre, kvw), BF16),
        ((pre, kvw), BF16),
        ((1, hd), F32),
        ((1, hd), F32),
    )
    results = pl.pallas_call(
        functools.partial(kernel, (n_dp, n_branch, inner, slots, rows, heads, group, pre, hd)),
        out_shape=tuple(pltpu.VMEM(*x) for x in shapes),
        in_specs=[hbm] * 6 + [vmem] * 2 + [smem] * 3,
        out_specs=(vmem,) * 8,
        scratch_shapes=[
            held(BF16, slots, rows, qw),
            held(BF16, slots, rows, qw),
            held(BF16, slots, rows, kvw),
            held(BF16, slots, rows, kvw),
            held(BF16, heads, pre, hd),
            *prefix_slots,
            held(BF16, n_branch, hd, pre),
            held(BF16, n_branch, hd, pre),
            held(F32, slots + 1, pre, hd),
            held(F32, slots + 1, pre, hd),
            held(F32, 2, pre, cols),
            held(BF16, 2, pre, cols),
            held(BF16, 2, pre, cols),
            held(F32, hd, cols),
            held(F32, hd, cols),
            held(BF16, heads, 6, pre, hd),
            held(BF16, heads, 6, pre, hd),
            held(F32, n_branch, 8, hd),
            held(F32, inner, 8, hd),
            held(F32, outer, 8, hd),
            held(F32, 8, hd),
            pltpu.SMEM((3, slots), jnp.int32),
            pltpu.SemaphoreType.DMA((heads, 6)),
            pltpu.SemaphoreType.DMA((heads, 6)),
            pltpu.SemaphoreType.DMA((heads, 6)),
            pltpu.SemaphoreType.DMA((heads, 6)),
            pltpu.SemaphoreType.DMA((4, 8)),
            pltpu.SemaphoreType.DMA((4, 8)),
            pltpu.SemaphoreType.DMA((2 * heads + 4,)),
            pltpu.SemaphoreType.REGULAR((2,)),
        ],
        compiler_params=pltpu.CompilerParams(
            collective_id=0, has_side_effects=True, vmem_limit_bytes=int(58 * 1024 * 1024)
        ),
    )(
        prefix_keys[0, 0], prefix_values[0, 0], resp_query[0, 0], resp_keys[0, 0],
        resp_values[0, 0], out_grad[0, 0], q_gain[None], k_gain[None],
        lengths[0, 0], slot_prompt[0, 0], prefix_owner[0],
    )
    outs = pl.pallas_call(
        write_out,
        out_shape=tuple(jax.ShapeDtypeStruct(*x) for x in shapes),
        in_specs=[vmem] * 8,
        out_specs=(hbm,) * 8,
        scratch_shapes=[pltpu.SemaphoreType.DMA((8,))],
        compiler_params=pltpu.CompilerParams(vmem_limit_bytes=4 * 1024 * 1024),
    )(*results)
    return tuple(x[None, None] for x in outs[:6]) + (outs[6][0], outs[7][0])


def solution(mesh):
    block = P("dp", "branch")
    return jax.shard_map(
        functools.partial(body, mesh.shape["dp"], mesh.shape["branch"]),
        mesh=mesh,
        in_specs=(block,) * 6 + (P(), P()) + (block, block, P("dp")),
        out_specs=(block,) * 6 + (P(), P()),
        check_vma=False,
    )
```

```python
import functools
import math

import jax
import jax.numpy as jnp
from jax import lax
from jax.experimental import pallas as pl
from jax.experimental.pallas import tpu as pltpu
from jax.sharding import PartitionSpec as P

EPSILON = 1e-06
MESH = pl.DeviceIdType.MESH
F32 = jnp.float32
BF16 = jnp.bfloat16
LOG2E = math.log2(math.e)
LN2 = math.log(2.0)


def dot(a, b):
    return lax.dot_general(a, b, (((1,), (0,)), ((), ())), preferred_element_type=F32)


def dot_nt(a, b):
    return lax.dot_general(a, b, (((1,), (1,)), ((), ())), preferred_element_type=F32)


def norm_parts(raw):
    vals = raw.astype(F32)
    inv = lax.rsqrt(jnp.mean(vals * vals, axis=-1, keepdims=True) + EPSILON)
    return vals * inv, inv


def kernel(
    dims,
    pk, pv, q, rk, rv, g, q_gain, k_gain, lengths, prompts, owners,
    attv, dqv, drkv, drvv, dpk, dpv, qg_out, kg_out,
    qv, gv, rkv, rvv, kraw,
    kb0, kb1, kb2, kb3, vb0, vb1, vb2, vb3,
    kt, vt, ck, cv, es, eb, ub, gq, gacc, rs_out, rs_in, ex1, ex2, ex3, ex4, meta,
    ag_send, ag_recv, rs_send, rs_recv, gx_send, gx_recv, load_sem, ready,
):
    n_dp, n_branch, inner, slots, rows, heads, group, pre, hd = dims
    outer = n_dp // inner
    kb, vb = (kb0, kb1, kb2, kb3), (vb0, vb1, vb2, vb3)
    width = group * hd
    cols = group * rows
    score_scale = 1.0 / math.sqrt(hd)

    me = lax.axis_index("branch")
    dp = lax.axis_index("dp")
    right = lax.rem(me + 1, n_branch)
    left = lax.rem(me + n_branch - 1, n_branch)
    in_c = lax.rem(dp, inner)
    out_c = dp // inner
    stages = (
        (ex2, in_c, inner, lambda k: {"dp": out_c * inner + lax.rem(in_c + k, inner)}),
        (ex3, out_c, outer, lambda k: {"dp": lax.rem(out_c + k, outer) * inner + in_c}),
    )
    met = inner + outer - 2

    barrier = pltpu.get_barrier_semaphore()

    def tell(sem, to):
        pl.semaphore_signal(sem, inc=1, device_id=to, device_id_type=MESH)

    @pl.when(me == 2)
    def _():
        tell(barrier, {"branch": 1})
        tell(barrier, {"branch": 3})

    @pl.when((me == 1) | (me == 3))
    def _():
        tell(barrier, {"branch": 2})

    @pl.when(me == 0)
    def _():
        for k in (1, 3, 2):
            tell(barrier, {"branch": k})
        for _, _, extent, partner in stages:
            for k in range(1, extent):
                tell(barrier, partner(k))

    def enter():
        @pl.when(me == 2)
        def _():
            pl.semaphore_wait(barrier, 3)
            tell(ready.at[1], {"branch": 0})

        @pl.when((me == 1) | (me == 3))
        def _():
            pl.semaphore_wait(barrier, 2)
            tell(ready.at[0], {"branch": 0})

        @pl.when(me == 0)
        def _():
            pl.semaphore_wait(ready.at[0], 2)

    def head_cols(h):
        return pl.ds(h * hd, hd)

    k_loads = [
        pltpu.make_async_copy(pk.at[:, head_cols(h)], kraw.at[h], load_sem.at[h])
        for h in range(heads)
    ]
    v_loads = [
        pltpu.make_async_copy(pv.at[:, head_cols(h)], vb[h].at[0], load_sem.at[heads + h])
        for h in range(heads)
    ]
    base = 2 * heads
    rest_loads = [
        pltpu.make_async_copy(src, dst, load_sem.at[base + i])
        for i, (src, dst) in enumerate(((q, qv), (g, gv), (rk, rkv), (rv, rvv)))
    ]
    for h in range(heads):
        k_loads[h].start()
        v_loads[h].start()
    for copy in rest_loads:
        copy.start()

    kg_row = k_gain[...]
    qg_row = q_gain[...]

    def own_hat(h):
        k_loads[h].wait()
        normed, _ = norm_parts(kraw[h])
        kb[h][0] = (normed * kg_row).astype(BF16)
        v_loads[h].wait()

    def remote(src, dst, send, recv, to):
        return pltpu.make_async_remote_copy(
            src_ref=src, dst_ref=dst, send_sem=send, recv_sem=recv,
            device_id={"branch": to}, device_id_type=MESH,
        )

    def ag(h, i):
        src, dst, to = (
            (kb[h].at[0], kb[h].at[3], right),
            (vb[h].at[0], vb[h].at[1], left),
            (vb[h].at[0], vb[h].at[3], right),
            (kb[h].at[0], kb[h].at[1], left),
            (kb[h].at[3], kb[h].at[2], right),
            (vb[h].at[1], vb[h].at[2], left),
        )[i]
        return remote(src, dst, ag_send.at[h, i], ag_recv.at[h, i], to)

    def ag_direct(h):
        for i in range(4):
            ag(h, i).start()

    def ag_forward(h):
        ag(h, 0).wait_recv()
        ag(h, 4).start()
        ag(h, 1).wait_recv()
        ag(h, 5).start()

    def ag_rest(h):
        for i in range(2, 6):
            ag(h, i).wait_recv()

    def rs(h, i):
        to = right if i % 2 == 0 else left
        return remote(rs_out.at[h, i], rs_in.at[h, i], rs_send.at[h, i], rs_recv.at[h, i], to)

    def rs_pack(h):
        for i, (acc, scale, r) in enumerate(
            ((ck, LN2, 2), (cv, 1.0, 2), (cv, 1.0, 1), (ck, LN2, 3), (ck, LN2, 1), (cv, 1.0, 3))
        ):
            rs_out[h, i] = (acc[meta[2, r]] * scale).astype(BF16)

    def rs_start(h):
        for i in range(4):
            rs(h, i).start()

    def rs_second(h):
        for i in (0, 1):
            rs(h, i).wait_recv()
            rs_out[h, 4 + i] = (rs_out[h, 4 + i].astype(F32) + rs_in[h, i].astype(F32)).astype(BF16)
            rs(h, 4 + i).start()

    def rs_final(h):
        for i in range(2, 6):
            rs(h, i).wait_recv()
        grad = rs_in[h, 3].astype(F32) + rs_in[h, 4].astype(F32)
        normed, inv = norm_parts(kraw[h])
        scaled = grad * kg_row
        back = inv * (scaled - normed * jnp.mean(scaled * normed, axis=-1, keepdims=True))
        dpk[:, h * hd : (h + 1) * hd] = back.astype(BF16)
        dpv[:, h * hd : (h + 1) * hd] = (rs_in[h, 2].astype(F32) + rs_in[h, 5].astype(F32)).astype(BF16)

    def transposes(h):
        for r in range(1, n_branch):
            kt[r] = kb[h][r].T
            vt[r] = vb[h][r].T

    block = 128
    lane = lax.broadcasted_iota(jnp.int32, (1, cols), 1)
    token = lane & (rows - 1)

    def slot_pass(s, h, u):
        rel = meta[0, s]
        prev = meta[1, s]
        live = token < lengths[s]
        at = [h * width + i * hd for i in range(group)]
        q_t = jnp.concatenate([qv[s, :, a : a + hd] for a in at], axis=0).T.astype(F32)
        g_t = jnp.concatenate([gv[s, :, a : a + hd] for a in at], axis=0).T.astype(F32)
        g_t = jnp.where(live, g_t, 0.0)
        g_low = g_t.astype(BF16)
        q_inv = lax.rsqrt(jnp.mean(q_t * q_t, axis=0, keepdims=True) + EPSILON)
        q_n = q_t * q_inv
        gain = gq[...]
        q_scaled = q_n * (gain * (LOG2E * score_scale))
        q_low = q_scaled.astype(BF16)
        k_n, k_inv = norm_parts(rkv[s, :, h * hd : (h + 1) * hd])
        k_low = (k_n * kg_row).astype(BF16)
        v_low = rvv[s, :, h * hd : (h + 1) * hd]

        allowed = lax.broadcasted_iota(jnp.int32, (rows, cols), 0) <= token
        e_r = jnp.where(allowed, jnp.exp2(dot(k_low, q_low)), 0.0)
        total = jnp.sum(e_r, axis=0, keepdims=True)
        for c in range(pre // block):
            part = pl.ds(c * block, block)
            e_c = jnp.exp2(dot(kb[h][rel, part, :], q_low))
            es[u, part, :] = e_c
            eb[u, part, :] = e_c.astype(BF16)
            total += jnp.sum(e_c, axis=0, keepdims=True)
        inv = 1.0 / total
        e_r_low = e_r.astype(BF16)
        o_t = (dot(vt[rel], eb[u]) + dot(v_low.T, e_r_low)) * inv
        dots = jnp.sum(g_t * o_t, axis=0, keepdims=True)
        o_low = jnp.where(live, o_t, 0.0).astype(BF16).T
        for i, a in enumerate(at):
            attv[s, :, a : a + hd] = o_low[i * rows : (i + 1) * rows, :]

        u_r = (e_r * (dot(v_low, g_low) - dots)).astype(BF16)
        for c in range(pre // block):
            part = pl.ds(c * block, block)
            d_c = dot(vb[h][rel, part, :], g_low)
            ub[u, part, :] = (es[u, part, :] * (d_c - dots)).astype(BF16)
        dq_t = (dot(kt[rel], ub[u]) + dot(k_low.T, u_r)) * (inv * score_scale)
        gacc[...] += q_n * dq_t
        scaled = gain * dq_t
        back = q_inv * (scaled - q_n * jnp.mean(scaled * q_n, axis=0, keepdims=True))
        back_low = back.astype(BF16).T
        for i, a in enumerate(at):
            dqv[s, :, a : a + hd] = back_low[i * rows : (i + 1) * rows, :]

        q_part = (q_scaled * inv).astype(BF16)
        g_part = (g_t * inv).astype(BF16)
        dk_r = dot_nt(u_r, q_part) * LN2
        scaled_k = dk_r * kg_row
        back_k = k_inv * (scaled_k - k_n * jnp.mean(scaled_k * k_n, axis=-1, keepdims=True))
        drkv[s, :, h * hd : (h + 1) * hd] = back_k.astype(BF16)
        drvv[s, :, h * hd : (h + 1) * hd] = dot_nt(e_r_low, g_part).astype(BF16)
        for c in range(pre // block):
            part = pl.ds(c * block, block)
            ck[s, part, :] = ck[prev, part, :] + dot_nt(ub[u, part, :], q_part)
            cv[s, part, :] = cv[prev, part, :] + dot_nt(eb[u, part, :], g_part)

    def run_head(h, events):
        def step(i, carry):
            for at, event in events:
                pl.when(i == at)(event)
            for u in range(2):
                slot_pass(2 * i + u, h, u)
            return carry

        lax.fori_loop(0, slots // 2, step, 0)

    own_hat(0)
    enter()
    ag_direct(0)
    own_hat(1)
    ag_forward(0)
    ag_direct(1)
    for h in range(2, heads):
        own_hat(h)

    rels = []
    for s in range(slots):
        rel = owners[prompts[s]] - me
        rel = jnp.where(rel < 0, rel + n_branch, rel)
        prev = jnp.int32(slots)
        for before in range(s):
            prev = jnp.where(rels[before] == rel, before, prev)
        rels.append(rel)
        meta[0, s] = rel
        meta[1, s] = prev
    for r in range(1, n_branch):
        last = jnp.int32(slots)
        for s in range(slots):
            last = jnp.where(rels[s] == r, s, last)
        meta[2, r] = last
    ck[slots] = jnp.zeros((pre, hd), F32)
    cv[slots] = jnp.zeros((pre, hd), F32)
    gq[...] = jnp.broadcast_to(qg_row, (cols, hd)).T
    gacc[...] = jnp.zeros_like(gacc)
    for copy in rest_loads:
        copy.wait()

    def gather_next(h):
        ag_forward(h)
        if h + 1 < heads:
            ag_direct(h + 1)
        else:
            for done in range(h - 1):
                rs_start(done)

    for h in range(heads):
        ag_rest(h)
        transposes(h)
        if h + 1 < heads:
            events = [(1, functools.partial(gather_next, h + 1))]
        else:
            events = [(2, functools.partial(rs_second, 0))]
        run_head(h, events)
        if h + 1 < heads:
            rs_pack(h)

    def spread(value):
        return jnp.broadcast_to(value, (8, hd))

    ex1[me] = spread(jnp.sum(gacc[...].T, axis=0, keepdims=True))

    def gain_copy(src, dst, i, k, j, to):
        return pltpu.make_async_remote_copy(
            src_ref=src, dst_ref=dst, send_sem=gx_send.at[i, k], recv_sem=gx_recv.at[i, j],
            device_id=to, device_id_type=MESH,
        )

    def up(place):
        return gain_copy(ex1.at[place], ex1.at[place], 0, 0, place, {"branch": 0})

    def down(k):
        return gain_copy(ex4, ex4, 3, k, 0, {"branch": k})

    def across(i, k):
        buf, place, _, partner = stages[i]
        return gain_copy(buf.at[place], buf.at[place], 1 + i, k, k, partner(k))

    def collect(buf, extent, copies):
        for copy in copies:
            copy.wait_recv()
        value = buf[0]
        for k in range(1, extent):
            value = value + buf[k]
        return value

    def send_across(i, value):
        buf, place, extent, _ = stages[i]
        buf[place] = value
        for k in range(1, extent):
            across(i, k).start()

    def collect_across(i):
        buf, _, extent, _ = stages[i]
        return collect(buf, extent, [across(i, k) for k in range(1, extent)])

    @pl.when(me != 0)
    def _():
        up(me).start()

    rs_second(heads - 3)
    rs_start(heads - 2)
    rs_pack(heads - 1)
    rs_start(heads - 1)

    @pl.when(me == 0)
    def _():
        value = collect(ex1, n_branch, [up(k) for k in range(1, n_branch)])
        pl.semaphore_wait(barrier, met)
        send_across(0, value)

    rs_final(heads - 4)
    rs_second(heads - 2)

    @pl.when(me == 0)
    def _():
        send_across(1, collect_across(0))

    rs_final(heads - 3)
    rs_second(heads - 1)

    @pl.when(me == 0)
    def _():
        ex4[...] = collect_across(1)
        pl.semaphore_wait(ready.at[1], 1)
        for k in range(1, n_branch):
            down(k).start()

    rs_final(heads - 2)
    rs_final(heads - 1)

    @pl.when(me != 0)
    def _():
        down(me).wait_recv()

    value = ex4[0:1, :]
    qg_out[...] = value
    kg_out[...] = value * qg_row / kg_row

    for h in range(heads):
        for i in range(6):
            ag(h, i).wait_send()
            rs(h, i).wait_send()

    @pl.when(me != 0)
    def _():
        up(me).wait_send()

    @pl.when(me == 0)
    def _():
        for i, (_, _, extent, _) in enumerate(stages):
            for k in range(1, extent):
                across(i, k).wait_send()
        for k in range(1, n_branch):
            down(k).wait_send()


def write_out(*refs):
    count = len(refs) // 2
    held, outs, sems = refs[:count], refs[count:-1], refs[-1]
    copies = [pltpu.make_async_copy(a, b, sems.at[i]) for i, (a, b) in enumerate(zip(held, outs))]
    for copy in copies:
        copy.start()
    for copy in copies:
        copy.wait()


def body(
    n_dp, n_branch,
    prefix_keys, prefix_values, resp_query, resp_keys, resp_values, out_grad,
    q_gain, k_gain, lengths, slot_prompt, prefix_owner,
):
    hd = q_gain.shape[0]
    pre, kvw = prefix_keys.shape[2:]
    slots, rows, qw = resp_query.shape[2:]
    heads = kvw // hd
    group = qw // kvw
    inner = math.gcd(n_dp, 8)
    outer = n_dp // inner
    cols = group * rows
    hbm = pl.BlockSpec(memory_space=pltpu.HBM)
    vmem = pl.BlockSpec(memory_space=pltpu.VMEM)
    smem = pl.BlockSpec(memory_space=pltpu.SMEM)

    def held(dtype, *shape):
        return pltpu.VMEM(shape, dtype)

    prefix_slots = [held(BF16, n_branch, pre, hd) for _ in range(2 * heads)]
    shapes = (
        ((slots, rows, qw), BF16),
        ((slots, rows, qw), BF16),
        ((slots, rows, kvw), BF16),
        ((slots, rows, kvw), BF16),
        ((pre, kvw), BF16),
        ((pre, kvw), BF16),
        ((1, hd), F32),
        ((1, hd), F32),
    )
    results = pl.pallas_call(
        functools.partial(kernel, (n_dp, n_branch, inner, slots, rows, heads, group, pre, hd)),
        out_shape=tuple(pltpu.VMEM(*x) for x in shapes),
        in_specs=[hbm] * 6 + [vmem] * 2 + [smem] * 3,
        out_specs=(vmem,) * 8,
        scratch_shapes=[
            held(BF16, slots, rows, qw),
            held(BF16, slots, rows, qw),
            held(BF16, slots, rows, kvw),
            held(BF16, slots, rows, kvw),
            held(BF16, heads, pre, hd),
            *prefix_slots,
            held(BF16, n_branch, hd, pre),
            held(BF16, n_branch, hd, pre),
            held(F32, slots + 1, pre, hd),
            held(F32, slots + 1, pre, hd),
            held(F32, 2, pre, cols),
            held(BF16, 2, pre, cols),
            held(BF16, 2, pre, cols),
            held(F32, hd, cols),
            held(F32, hd, cols),
            held(BF16, heads, 6, pre, hd),
            held(BF16, heads, 6, pre, hd),
            held(F32, n_branch, 8, hd),
            held(F32, inner, 8, hd),
            held(F32, outer, 8, hd),
            held(F32, 8, hd),
            pltpu.SMEM((3, slots), jnp.int32),
            pltpu.SemaphoreType.DMA((heads, 6)),
            pltpu.SemaphoreType.DMA((heads, 6)),
            pltpu.SemaphoreType.DMA((heads, 6)),
            pltpu.SemaphoreType.DMA((heads, 6)),
            pltpu.SemaphoreType.DMA((4, 8)),
            pltpu.SemaphoreType.DMA((4, 8)),
            pltpu.SemaphoreType.DMA((2 * heads + 4,)),
            pltpu.SemaphoreType.REGULAR((2,)),
        ],
        compiler_params=pltpu.CompilerParams(
            collective_id=0, has_side_effects=True, vmem_limit_bytes=int(58 * 1024 * 1024)
        ),
    )(
        prefix_keys[0, 0], prefix_values[0, 0], resp_query[0, 0], resp_keys[0, 0],
        resp_values[0, 0], out_grad[0, 0], q_gain[None], k_gain[None],
        lengths[0, 0], slot_prompt[0, 0], prefix_owner[0],
    )
    outs = pl.pallas_call(
        write_out,
        out_shape=tuple(jax.ShapeDtypeStruct(*x) for x in shapes),
        in_specs=[vmem] * 8,
        out_specs=(hbm,) * 8,
        scratch_shapes=[pltpu.SemaphoreType.DMA((8,))],
        compiler_params=pltpu.CompilerParams(vmem_limit_bytes=4 * 1024 * 1024),
    )(*results)
    return tuple(x[None, None] for x in outs[:6]) + (outs[6][0], outs[7][0])


def solution(mesh):
    block = P("dp", "branch")
    return jax.shard_map(
        functools.partial(body, mesh.shape["dp"], mesh.shape["branch"]),
        mesh=mesh,
        in_specs=(block,) * 6 + (P(), P()) + (block, block, P("dp")),
        out_specs=(block,) * 6 + (P(), P()),
        check_vma=False,
    )
```

```python
import functools
import math

import jax
import jax.numpy as jnp
from jax import lax
from jax.experimental import pallas as pl
from jax.experimental.pallas import tpu as pltpu
from jax.sharding import PartitionSpec as P

EPSILON = 1e-06
MESH = pl.DeviceIdType.MESH
F32 = jnp.float32
BF16 = jnp.bfloat16
LOG2E = math.log2(math.e)
LN2 = math.log(2.0)


def dot(a, b):
    return lax.dot_general(a, b, (((1,), (0,)), ((), ())), preferred_element_type=F32)


def dot_nt(a, b):
    return lax.dot_general(a, b, (((1,), (1,)), ((), ())), preferred_element_type=F32)


def norm_parts(raw):
    vals = raw.astype(F32)
    inv = lax.rsqrt(jnp.mean(vals * vals, axis=-1, keepdims=True) + EPSILON)
    return vals * inv, inv


def norm_back(scaled, normed):
    return scaled - normed * jnp.mean(scaled * normed, axis=-1, keepdims=True)


def kernel(
    dims,
    pk, pv, q, rk, rv, g, q_gain, k_gain, lengths_in, prompts_in, owners_in,
    attv, dqv, drkv, drvv, dpk, dpv, qg_out, kg_out, tail,
    qv, gv, rkv, rvv, kraw,
    kb0, kb1, kb2, kb3, vb0, vb1, vb2, vb3,
    kt, vt, ck, cv, es, eb, ub, gq, gacc, rs_out, rs_in, ex1, ex2, ex3, ex4, gains, lengths, prompts, owners, meta,
    ag_send, ag_recv, rs_send, rs_recv, gx_send, gx_recv, load_sem, ready,
):
    n_dp, n_branch, inner, slots, rows, heads, group, pre, hd = dims
    outer = n_dp // inner
    kb, vb = (kb0, kb1, kb2, kb3), (vb0, vb1, vb2, vb3)
    width = group * hd
    cols = group * rows
    score_scale = 1.0 / math.sqrt(hd)

    me = lax.axis_index("branch")
    dp = lax.axis_index("dp")
    right = lax.rem(me + 1, n_branch)
    left = lax.rem(me + n_branch - 1, n_branch)
    in_c = lax.rem(dp, inner)
    out_c = dp // inner
    stages = (
        (ex2, in_c, inner, lambda k: {"dp": out_c * inner + lax.rem(in_c + k, inner)}),
        (ex3, out_c, outer, lambda k: {"dp": lax.rem(out_c + k, outer) * inner + in_c}),
    )
    met = inner + outer - 2

    barrier = pltpu.get_barrier_semaphore()

    def tell(sem, to):
        pl.semaphore_signal(sem, inc=1, device_id=to, device_id_type=MESH)

    @pl.when(me == 2)
    def _():
        tell(barrier, {"branch": 1})
        tell(barrier, {"branch": 3})

    @pl.when((me == 1) | (me == 3))
    def _():
        tell(barrier, {"branch": 2})

    @pl.when(me == 0)
    def _():
        for k in (1, 3, 2):
            tell(barrier, {"branch": k})

    def greet_far():
        @pl.when(me == 0)
        def _():
            for _, _, extent, partner in stages:
                for k in range(1, extent):
                    tell(barrier, partner(k))

    def answer():
        @pl.when(me == 2)
        def _():
            pl.semaphore_wait(barrier, 3)
            tell(ready.at[1], {"branch": 0})

        @pl.when((me == 1) | (me == 3))
        def _():
            pl.semaphore_wait(barrier, 2)
            tell(ready.at[0], {"branch": 0})

    def enter():
        @pl.when(me == 0)
        def _():
            pl.semaphore_wait(ready.at[0], 2)

    def head_cols(h):
        return pl.ds(h * hd, hd)

    k_loads = [
        pltpu.make_async_copy(pk.at[:, head_cols(h)], kraw.at[h], load_sem.at[h])
        for h in range(heads)
    ]
    v_loads = [
        pltpu.make_async_copy(pv.at[:, head_cols(h)], vb[h].at[0], load_sem.at[heads + h])
        for h in range(heads)
    ]
    base = 2 * heads
    rest_loads = [
        pltpu.make_async_copy(src, dst, load_sem.at[base + i])
        for i, (src, dst) in enumerate(((q, qv), (g, gv), (rk, rkv), (rv, rvv)))
    ]
    small_loads = [
        pltpu.make_async_copy(src, dst, load_sem.at[base + 4 + i])
        for i, (src, dst) in enumerate(
            (
                (k_gain, gains.at[pl.ds(0, 1)]),
                (q_gain, gains.at[pl.ds(8, 1)]),
                (lengths_in, lengths),
                (prompts_in, prompts),
                (owners_in, owners),
            )
        )
    ]
    k_loads[0].start()
    small_loads[0].start()
    v_loads[0].start()
    for copy in small_loads[1:]:
        copy.start()
    for h in range(1, heads):
        k_loads[h].start()
        v_loads[h].start()
    for copy in rest_loads:
        copy.start()
    small_loads[0].wait()
    kg_row = gains[0:1, :]

    def own_hat(h):
        k_loads[h].wait()
        normed, _ = norm_parts(kraw[h])
        kb[h][0] = (normed * kg_row).astype(BF16)
        v_loads[h].wait()

    def remote(src, dst, send, recv, to):
        return pltpu.make_async_remote_copy(
            src_ref=src, dst_ref=dst, send_sem=send, recv_sem=recv,
            device_id={"branch": to}, device_id_type=MESH,
        )

    def ag(h, i):
        src, dst, to = (
            (kb[h].at[0], kb[h].at[3], right),
            (vb[h].at[0], vb[h].at[1], left),
            (vb[h].at[0], vb[h].at[3], right),
            (kb[h].at[0], kb[h].at[1], left),
            (kb[h].at[3], kb[h].at[2], right),
            (vb[h].at[1], vb[h].at[2], left),
        )[i]
        return remote(src, dst, ag_send.at[h, i], ag_recv.at[h, i], to)

    def ag_direct(h):
        for i in range(4):
            ag(h, i).start()

    def ag_forward(h):
        ag(h, 0).wait_recv()
        ag(h, 4).start()
        ag(h, 1).wait_recv()
        ag(h, 5).start()

    def ag_rest(h):
        for i in range(2, 6):
            ag(h, i).wait_recv()

    def rs(h, i):
        to = right if i % 2 == 0 else left
        return remote(rs_out.at[h, i], rs_in.at[h, i], rs_send.at[h, i], rs_recv.at[h, i], to)

    def rs_pack(h):
        for i, (acc, scale, r) in enumerate(
            ((ck, LN2, 2), (cv, 1.0, 2), (cv, 1.0, 1), (ck, LN2, 3), (ck, LN2, 1), (cv, 1.0, 3))
        ):
            rs_out[h, i] = (acc[meta[2, r]] * scale).astype(BF16)

    def rs_start(h):
        for i in range(4):
            rs(h, i).start()

    def rs_second(h):
        for i in (0, 1):
            rs(h, i).wait_recv()
            rs_out[h, 4 + i] = (rs_out[h, 4 + i].astype(F32) + rs_in[h, i].astype(F32)).astype(BF16)
            rs(h, 4 + i).start()

    def rs_final(h):
        normed, inv = norm_parts(kraw[h])
        if h == heads - 1:
            tail[1] = normed
        for i in range(2, 6):
            rs(h, i).wait_recv()
        scaled = (rs_in[h, 3].astype(F32) + rs_in[h, 4].astype(F32)) * (inv * kg_row)
        if h == heads - 1:
            tail[0] = scaled
        else:
            dpk[:, h * hd : (h + 1) * hd] = norm_back(scaled, normed).astype(BF16)
        dpv[:, h * hd : (h + 1) * hd] = (rs_in[h, 2].astype(F32) + rs_in[h, 5].astype(F32)).astype(BF16)

    def transposes(h):
        for r in range(1, n_branch):
            kt[r] = kb[h][r].T
            vt[r] = vb[h][r].T

    block = 128
    lane = lax.broadcasted_iota(jnp.int32, (1, cols), 1)
    token = lane & (rows - 1)

    def slot_pass(s, h, u):
        rel = meta[0, s]
        prev = meta[1, s]
        live = token < lengths[s]
        at = [h * width + i * hd for i in range(group)]
        q_t = jnp.concatenate([qv[s, :, a : a + hd] for a in at], axis=0).T.astype(F32)
        g_t = jnp.concatenate([gv[s, :, a : a + hd] for a in at], axis=0).T.astype(F32)
        g_t = jnp.where(live, g_t, 0.0)
        g_low = g_t.astype(BF16)
        q_inv = lax.rsqrt(jnp.mean(q_t * q_t, axis=0, keepdims=True) + EPSILON)
        q_n = q_t * q_inv
        gain = gq[...]
        q_scaled = q_n * (gain * (LOG2E * score_scale))
        q_low = q_scaled.astype(BF16)
        k_n, k_inv = norm_parts(rkv[s, :, h * hd : (h + 1) * hd])
        k_low = (k_n * kg_row).astype(BF16)
        v_low = rvv[s, :, h * hd : (h + 1) * hd]

        allowed = lax.broadcasted_iota(jnp.int32, (rows, cols), 0) <= token
        e_r = jnp.where(allowed, jnp.exp2(dot(k_low, q_low)), 0.0)
        total = jnp.sum(e_r, axis=0, keepdims=True)
        for c in range(pre // block):
            part = pl.ds(c * block, block)
            e_c = jnp.exp2(dot(kb[h][rel, part, :], q_low))
            es[u, part, :] = e_c
            eb[u, part, :] = e_c.astype(BF16)
            total += jnp.sum(e_c, axis=0, keepdims=True)
        inv = 1.0 / total
        e_r_low = e_r.astype(BF16)
        o_t = (dot(vt[rel], eb[u]) + dot(v_low.T, e_r_low)) * inv
        dots = jnp.sum(g_t * o_t, axis=0, keepdims=True)
        o_low = jnp.where(live, o_t, 0.0).astype(BF16).T
        for i, a in enumerate(at):
            attv[s, :, a : a + hd] = o_low[i * rows : (i + 1) * rows, :]

        u_r = (e_r * (dot(v_low, g_low) - dots)).astype(BF16)
        for c in range(pre // block):
            part = pl.ds(c * block, block)
            d_c = dot(vb[h][rel, part, :], g_low)
            ub[u, part, :] = (es[u, part, :] * (d_c - dots)).astype(BF16)
        dq_t = (dot(kt[rel], ub[u]) + dot(k_low.T, u_r)) * (inv * score_scale)
        gacc[...] += q_n * dq_t
        scaled = gain * dq_t
        back = q_inv * (scaled - q_n * jnp.mean(scaled * q_n, axis=0, keepdims=True))
        back_low = back.astype(BF16).T
        for i, a in enumerate(at):
            dqv[s, :, a : a + hd] = back_low[i * rows : (i + 1) * rows, :]

        q_part = (q_scaled * inv).astype(BF16)
        g_part = (g_t * inv).astype(BF16)
        dk_r = dot_nt(u_r, q_part) * LN2
        scaled_k = dk_r * kg_row
        back_k = k_inv * (scaled_k - k_n * jnp.mean(scaled_k * k_n, axis=-1, keepdims=True))
        drkv[s, :, h * hd : (h + 1) * hd] = back_k.astype(BF16)
        drvv[s, :, h * hd : (h + 1) * hd] = dot_nt(e_r_low, g_part).astype(BF16)
        for c in range(pre // block):
            part = pl.ds(c * block, block)
            ck[s, part, :] = ck[prev, part, :] + dot_nt(ub[u, part, :], q_part)
            cv[s, part, :] = cv[prev, part, :] + dot_nt(eb[u, part, :], g_part)

    def run_head(h, events):
        def step(i, carry):
            for at, event in events:
                pl.when(i == at)(event)
            for u in range(2):
                slot_pass(2 * i + u, h, u)
            return carry

        lax.fori_loop(0, slots // 2, step, 0)

    answer()
    own_hat(0)
    enter()
    ag_direct(0)
    greet_far()
    own_hat(1)
    ag_forward(0)
    ag_direct(1)
    for h in range(2, heads):
        own_hat(h)

    for copy in small_loads[1:]:
        copy.wait()
    qg_row = gains[8:9, :]
    rels = []
    for s in range(slots):
        rel = owners[prompts[s]] - me
        rel = jnp.where(rel < 0, rel + n_branch, rel)
        prev = jnp.int32(slots)
        for before in range(s):
            prev = jnp.where(rels[before] == rel, before, prev)
        rels.append(rel)
        meta[0, s] = rel
        meta[1, s] = prev
    for r in range(1, n_branch):
        last = jnp.int32(slots)
        for s in range(slots):
            last = jnp.where(rels[s] == r, s, last)
        meta[2, r] = last
    ck[slots] = jnp.zeros((pre, hd), F32)
    cv[slots] = jnp.zeros((pre, hd), F32)
    gq[...] = jnp.broadcast_to(qg_row, (cols, hd)).T
    gacc[...] = jnp.zeros_like(gacc)
    for copy in rest_loads:
        copy.wait()

    def gather_next(h):
        ag_forward(h)
        if h + 1 < heads:
            ag_direct(h + 1)
        else:
            for done in range(h - 1):
                rs_start(done)

    for h in range(heads):
        ag_rest(h)
        transposes(h)
        if h + 1 < heads:
            events = [(1, functools.partial(gather_next, h + 1))]
        else:
            events = [(2, functools.partial(rs_second, 0))]
        run_head(h, events)
        if h + 1 < heads:
            rs_pack(h)

    def spread(value):
        return jnp.broadcast_to(value, (8, hd))

    ex1[me] = spread(jnp.sum(gacc[...].T, axis=0, keepdims=True))

    def gain_copy(src, dst, i, k, j, to):
        return pltpu.make_async_remote_copy(
            src_ref=src, dst_ref=dst, send_sem=gx_send.at[i, k], recv_sem=gx_recv.at[i, j],
            device_id=to, device_id_type=MESH,
        )

    def up(place):
        return gain_copy(ex1.at[place], ex1.at[place], 0, 0, place, {"branch": 0})

    def down(k):
        return gain_copy(ex4, ex4, 3, k, 0, {"branch": k})

    def across(i, k):
        buf, place, _, partner = stages[i]
        return gain_copy(buf.at[place], buf.at[place], 1 + i, k, k, partner(k))

    def collect(buf, extent, copies):
        for copy in copies:
            copy.wait_recv()
        value = buf[0]
        for k in range(1, extent):
            value = value + buf[k]
        return value

    def send_across(i, value):
        buf, place, extent, _ = stages[i]
        buf[place] = value
        for k in range(1, extent):
            across(i, k).start()

    def collect_across(i):
        buf, _, extent, _ = stages[i]
        return collect(buf, extent, [across(i, k) for k in range(1, extent)])

    @pl.when(me != 0)
    def _():
        up(me).start()

    rs_second(heads - 3)
    rs_start(heads - 2)
    rs_pack(heads - 1)
    rs_start(heads - 1)

    @pl.when(me == 0)
    def _():
        value = collect(ex1, n_branch, [up(k) for k in range(1, n_branch)])
        pl.semaphore_wait(barrier, met)
        send_across(0, value)

    rs_final(heads - 4)
    rs_second(heads - 2)

    @pl.when(me == 0)
    def _():
        send_across(1, collect_across(0))

    rs_final(heads - 3)
    rs_second(heads - 1)

    @pl.when(me == 0)
    def _():
        ex4[...] = collect_across(1)
        pl.semaphore_wait(ready.at[1], 1)
        for k in range(1, n_branch):
            down(k).start()

    rs_final(heads - 2)
    rs_final(heads - 1)

    @pl.when(me != 0)
    def _():
        down(me).wait_recv()

    value = ex4[0:1, :]
    qg_out[...] = value
    kg_out[...] = value * qg_row / kg_row

    for h in range(heads):
        for i in range(6):
            ag(h, i).wait_send()
            rs(h, i).wait_send()

    @pl.when(me != 0)
    def _():
        up(me).wait_send()

    @pl.when(me == 0)
    def _():
        for i, (_, _, extent, _) in enumerate(stages):
            for k in range(1, extent):
                across(i, k).wait_send()
        for k in range(1, n_branch):
            down(k).wait_send()


def write_out(*refs):
    count = (len(refs) - 3) // 2
    held, last, outs, own, sems = refs[:count], refs[count], refs[count + 1 : -2], refs[-2], refs[-1]
    early = held[4].shape[1] - own.shape[1]
    pairs = list(zip(held, outs))
    pairs[4] = (held[4].at[:, pl.ds(0, early)], outs[4].at[:, pl.ds(0, early)])
    copies = [pltpu.make_async_copy(a, b, sems.at[i]) for i, (a, b) in enumerate(pairs)]
    for copy in copies:
        copy.start()
    own[...] = norm_back(last[0], last[1]).astype(BF16)
    copies.append(
        pltpu.make_async_copy(own, outs[4].at[:, pl.ds(early, own.shape[1])], sems.at[count])
    )
    copies[-1].start()
    for copy in copies:
        copy.wait()


def body(
    n_dp, n_branch,
    prefix_keys, prefix_values, resp_query, resp_keys, resp_values, out_grad,
    q_gain, k_gain, lengths, slot_prompt, prefix_owner,
):
    hd = q_gain.shape[0]
    pre, kvw = prefix_keys.shape[2:]
    slots, rows, qw = resp_query.shape[2:]
    heads = kvw // hd
    group = qw // kvw
    inner = math.gcd(n_dp, 8)
    outer = n_dp // inner
    cols = group * rows
    hbm = pl.BlockSpec(memory_space=pltpu.HBM)
    vmem = pl.BlockSpec(memory_space=pltpu.VMEM)

    def held(dtype, *shape):
        return pltpu.VMEM(shape, dtype)

    prefix_slots = [held(BF16, n_branch, pre, hd) for _ in range(2 * heads)]
    shapes = (
        ((slots, rows, qw), BF16),
        ((slots, rows, qw), BF16),
        ((slots, rows, kvw), BF16),
        ((slots, rows, kvw), BF16),
        ((pre, kvw), BF16),
        ((pre, kvw), BF16),
        ((1, hd), F32),
        ((1, hd), F32),
    )
    results = pl.pallas_call(
        functools.partial(kernel, (n_dp, n_branch, inner, slots, rows, heads, group, pre, hd)),
        out_shape=tuple(pltpu.VMEM(*x) for x in shapes) + (pltpu.VMEM((2, pre, hd), F32),),
        in_specs=[hbm] * 11,
        out_specs=(vmem,) * 9,
        scratch_shapes=[
            held(BF16, slots, rows, qw),
            held(BF16, slots, rows, qw),
            held(BF16, slots, rows, kvw),
            held(BF16, slots, rows, kvw),
            held(BF16, heads, pre, hd),
            *prefix_slots,
            held(BF16, n_branch, hd, pre),
            held(BF16, n_branch, hd, pre),
            held(F32, slots + 1, pre, hd),
            held(F32, slots + 1, pre, hd),
            held(F32, 2, pre, cols),
            held(BF16, 2, pre, cols),
            held(BF16, 2, pre, cols),
            held(F32, hd, cols),
            held(F32, hd, cols),
            held(BF16, heads, 6, pre, hd),
            held(BF16, heads, 6, pre, hd),
            held(F32, n_branch, 8, hd),
            held(F32, inner, 8, hd),
            held(F32, outer, 8, hd),
            held(F32, 8, hd),
            held(F32, 16, hd),
            pltpu.SMEM((slots,), jnp.int32),
            pltpu.SMEM((slots,), jnp.int32),
            pltpu.SMEM((n_branch,), jnp.int32),
            pltpu.SMEM((3, slots), jnp.int32),
            pltpu.SemaphoreType.DMA((heads, 6)),
            pltpu.SemaphoreType.DMA((heads, 6)),
            pltpu.SemaphoreType.DMA((heads, 6)),
            pltpu.SemaphoreType.DMA((heads, 6)),
            pltpu.SemaphoreType.DMA((4, 8)),
            pltpu.SemaphoreType.DMA((4, 8)),
            pltpu.SemaphoreType.DMA((2 * heads + 9,)),
            pltpu.SemaphoreType.REGULAR((2,)),
        ],
        compiler_params=pltpu.CompilerParams(
            collective_id=0, has_side_effects=True, vmem_limit_bytes=57 * 1024 * 1024
        ),
    )(
        prefix_keys[0, 0], prefix_values[0, 0], resp_query[0, 0], resp_keys[0, 0],
        resp_values[0, 0], out_grad[0, 0], q_gain[None], k_gain[None],
        lengths[0, 0], slot_prompt[0, 0], prefix_owner[0],
    )
    outs = pl.pallas_call(
        write_out,
        out_shape=tuple(jax.ShapeDtypeStruct(*x) for x in shapes),
        in_specs=[vmem] * 9,
        out_specs=(hbm,) * 8,
        scratch_shapes=[held(BF16, pre, hd), pltpu.SemaphoreType.DMA((9,))],
        compiler_params=pltpu.CompilerParams(vmem_limit_bytes=4 * 1024 * 1024),
    )(*results)
    return tuple(x[None, None] for x in outs[:6]) + (outs[6][0], outs[7][0])


def solution(mesh):
    block = P("dp", "branch")
    return jax.shard_map(
        functools.partial(body, mesh.shape["dp"], mesh.shape["branch"]),
        mesh=mesh,
        in_specs=(block,) * 6 + (P(), P()) + (block, block, P("dp")),
        out_specs=(block,) * 6 + (P(), P()),
        check_vma=False,
    )
```

```python
import functools
import math

import jax
import jax.numpy as jnp
from jax import lax
from jax.experimental import pallas as pl
from jax.experimental.pallas import tpu as pltpu
from jax.sharding import PartitionSpec as P

EPSILON = 1e-06
MESH = pl.DeviceIdType.MESH
F32 = jnp.float32
BF16 = jnp.bfloat16
LOG2E = math.log2(math.e)


def dot(a, b):
    return lax.dot_general(a, b, (((1,), (0,)), ((), ())), preferred_element_type=F32)


def dot_nt(a, b):
    return lax.dot_general(a, b, (((1,), (1,)), ((), ())), preferred_element_type=F32)


def norm_parts(raw):
    vals = raw.astype(F32)
    inv = lax.rsqrt(jnp.mean(vals * vals, axis=-1, keepdims=True) + EPSILON)
    return vals * inv, inv


def norm_back(scaled, normed):
    return scaled - normed * jnp.mean(scaled * normed, axis=-1, keepdims=True)


def kernel(
    dims,
    pk, pv, q, rk, rv, g, q_gain, k_gain, lengths_in, prompts_in, owners_in,
    attv, dqv, drkv, drvv, dpk, dpv, qg_out, kg_out, tail,
    qv, gv, rkv, rvv, kraw,
    kb0, kb1, kb2, kb3, vb0, vb1, vb2, vb3,
    kt, vt, ck, cv, es, ds, eb, ub, gq, gacc, rs_out, rs_in, ex1, ex2, ex3, ex4, gains, lengths, prompts, owners, meta,
    ag_send, ag_recv, rs_send, rs_recv, gx_send, gx_recv, load_sem, ready,
):
    n_dp, n_branch, inner, slots, rows, heads, group, pre, hd = dims
    outer = n_dp // inner
    kb, vb = (kb0, kb1, kb2, kb3), (vb0, vb1, vb2, vb3)
    width = group * hd
    cols = group * rows
    score_scale = 1.0 / math.sqrt(hd)

    me = lax.axis_index("branch")
    dp = lax.axis_index("dp")
    right = lax.rem(me + 1, n_branch)
    left = lax.rem(me + n_branch - 1, n_branch)
    in_c = lax.rem(dp, inner)
    out_c = dp // inner
    stages = (
        (ex2, in_c, inner, lambda k: {"dp": out_c * inner + lax.rem(in_c + k, inner)}),
        (ex3, out_c, outer, lambda k: {"dp": lax.rem(out_c + k, outer) * inner + in_c}),
    )
    met = inner + outer - 2

    barrier = pltpu.get_barrier_semaphore()

    def tell(sem, to):
        pl.semaphore_signal(sem, inc=1, device_id=to, device_id_type=MESH)

    @pl.when(me == 2)
    def _():
        tell(barrier, {"branch": 1})
        tell(barrier, {"branch": 3})

    @pl.when((me == 1) | (me == 3))
    def _():
        tell(barrier, {"branch": 2})

    @pl.when(me == 0)
    def _():
        for k in (1, 3, 2):
            tell(barrier, {"branch": k})

    def greet_far():
        @pl.when(me == 0)
        def _():
            for _, _, extent, partner in stages:
                for k in range(1, extent):
                    tell(barrier, partner(k))

    def answer():
        @pl.when(me == 2)
        def _():
            pl.semaphore_wait(barrier, 3)
            tell(ready.at[1], {"branch": 0})

        @pl.when((me == 1) | (me == 3))
        def _():
            pl.semaphore_wait(barrier, 2)
            tell(ready.at[0], {"branch": 0})

    def enter():
        @pl.when(me == 0)
        def _():
            pl.semaphore_wait(ready.at[0], 2)

    def head_cols(h):
        return pl.ds(h * hd, hd)

    k_loads = [
        pltpu.make_async_copy(pk.at[:, head_cols(h)], kraw.at[h], load_sem.at[h])
        for h in range(heads)
    ]
    v_loads = [
        pltpu.make_async_copy(pv.at[:, head_cols(h)], vb[h].at[0], load_sem.at[heads + h])
        for h in range(heads)
    ]
    base = 2 * heads
    rest_loads = [
        pltpu.make_async_copy(src, dst, load_sem.at[base + i])
        for i, (src, dst) in enumerate(((q, qv), (g, gv), (rk, rkv), (rv, rvv)))
    ]
    small_loads = [
        pltpu.make_async_copy(src, dst, load_sem.at[base + 4 + i])
        for i, (src, dst) in enumerate(
            (
                (k_gain, gains.at[pl.ds(0, 1)]),
                (q_gain, gains.at[pl.ds(8, 1)]),
                (lengths_in, lengths),
                (prompts_in, prompts),
                (owners_in, owners),
            )
        )
    ]
    k_loads[0].start()
    small_loads[0].start()
    v_loads[0].start()
    for copy in small_loads[1:]:
        copy.start()
    for h in range(1, heads):
        k_loads[h].start()
        v_loads[h].start()
    for copy in rest_loads:
        copy.start()
    small_loads[0].wait()
    kg_row = gains[0:1, :]

    def own_hat(h):
        k_loads[h].wait()
        normed, _ = norm_parts(kraw[h])
        kb[h][0] = (normed * kg_row).astype(BF16)
        v_loads[h].wait()

    def remote(src, dst, send, recv, to):
        return pltpu.make_async_remote_copy(
            src_ref=src, dst_ref=dst, send_sem=send, recv_sem=recv,
            device_id={"branch": to}, device_id_type=MESH,
        )

    def ag(h, i):
        src, dst, to = (
            (kb[h].at[0], kb[h].at[3], right),
            (vb[h].at[0], vb[h].at[1], left),
            (vb[h].at[0], vb[h].at[3], right),
            (kb[h].at[0], kb[h].at[1], left),
            (kb[h].at[3], kb[h].at[2], right),
            (vb[h].at[1], vb[h].at[2], left),
        )[i]
        return remote(src, dst, ag_send.at[h, i], ag_recv.at[h, i], to)

    def ag_direct(h):
        for i in range(4):
            ag(h, i).start()

    def ag_forward(h):
        ag(h, 0).wait_recv()
        ag(h, 4).start()
        ag(h, 1).wait_recv()
        ag(h, 5).start()

    def ag_rest(h):
        for i in range(2, 6):
            ag(h, i).wait_recv()

    def rs(h, i):
        to = right if i % 2 == 0 else left
        return remote(rs_out.at[h, i], rs_in.at[h, i], rs_send.at[h, i], rs_recv.at[h, i], to)

    def rs_pack(h):
        for i, (acc, r) in enumerate(((ck, 2), (cv, 2), (cv, 1), (ck, 3), (ck, 1), (cv, 3))):
            rs_out[h, i] = acc[meta[2, r]].astype(BF16)

    def rs_start(h):
        for i in range(4):
            rs(h, i).start()

    def rs_second(h):
        for i in (0, 1):
            rs(h, i).wait_recv()
            rs_out[h, 4 + i] = (rs_out[h, 4 + i].astype(F32) + rs_in[h, i].astype(F32)).astype(BF16)
            rs(h, 4 + i).start()

    def rs_final(h):
        normed, inv = norm_parts(kraw[h])
        if h == heads - 1:
            tail[1] = normed
        for i in range(2, 6):
            rs(h, i).wait_recv()
        scaled = (rs_in[h, 3].astype(F32) + rs_in[h, 4].astype(F32)) * (inv * kg_row)
        if h == heads - 1:
            tail[0] = scaled
        else:
            dpk[:, h * hd : (h + 1) * hd] = norm_back(scaled, normed).astype(BF16)
        dpv[:, h * hd : (h + 1) * hd] = (rs_in[h, 2].astype(F32) + rs_in[h, 5].astype(F32)).astype(BF16)

    def transposes(h):
        for r in range(1, n_branch):
            kt[r] = kb[h][r].T
            vt[r] = vb[h][r].T

    block = 128
    lane = lax.broadcasted_iota(jnp.int32, (1, cols), 1)
    token = lane & (rows - 1)

    def slot_pass(s, h, u):
        rel = meta[0, s]
        prev = meta[1, s]
        live = token < lengths[s]
        at = [h * width + i * hd for i in range(group)]
        q_t = jnp.concatenate([qv[s, :, a : a + hd] for a in at], axis=0).T.astype(F32)
        g_t = jnp.concatenate([gv[s, :, a : a + hd] for a in at], axis=0).T.astype(F32)
        g_t = jnp.where(live, g_t, 0.0)
        g_low = g_t.astype(BF16)
        q_inv = lax.rsqrt(jnp.mean(q_t * q_t, axis=0, keepdims=True) + EPSILON)
        q_n = q_t * q_inv
        gain = gq[...]
        q_low = (q_n * gain).astype(BF16)
        k_n, k_inv = norm_parts(rkv[s, :, h * hd : (h + 1) * hd])
        k_low = (k_n * kg_row).astype(BF16)
        v_low = rvv[s, :, h * hd : (h + 1) * hd]

        allowed = lax.broadcasted_iota(jnp.int32, (rows, cols), 0) <= token
        e_r = jnp.where(allowed, jnp.exp2(dot(k_low, q_low) * (LOG2E * score_scale)), 0.0)
        d_r = dot(v_low, g_low)
        total = jnp.sum(e_r, axis=0, keepdims=True)
        mixed = jnp.sum(e_r * d_r, axis=0, keepdims=True)
        for c in range(pre // block):
            part = pl.ds(c * block, block)
            e_c = jnp.exp2(dot(kb[h][rel, part, :], q_low) * (LOG2E * score_scale))
            d_c = dot(vb[h][rel, part, :], g_low)
            es[u, part, :] = e_c
            ds[u, part, :] = d_c
            total += jnp.sum(e_c, axis=0, keepdims=True)
            mixed += jnp.sum(e_c * d_c, axis=0, keepdims=True)
        inv = 1.0 / total
        mixed = mixed * inv
        scaled_inv = inv * score_scale
        p_r = (e_r * inv).astype(BF16)
        u_r = (e_r * scaled_inv * (d_r - mixed)).astype(BF16)
        for c in range(pre // block):
            part = pl.ds(c * block, block)
            e_c = es[u, part, :]
            eb[u, part, :] = (e_c * inv).astype(BF16)
            ub[u, part, :] = (e_c * scaled_inv * (ds[u, part, :] - mixed)).astype(BF16)

        o_t = dot(vt[rel], eb[u]) + dot(v_low.T, p_r)
        o_low = jnp.where(live, o_t, 0.0).astype(BF16).T
        for i, a in enumerate(at):
            attv[s, :, a : a + hd] = o_low[i * rows : (i + 1) * rows, :]
        dq_t = dot(kt[rel], ub[u]) + dot(k_low.T, u_r)
        gacc[0] += q_n * dq_t
        gacc[1] += q_low.astype(F32) * dq_t
        scaled = gain * dq_t
        back = q_inv * (scaled - q_n * jnp.mean(scaled * q_n, axis=0, keepdims=True))
        back_low = back.astype(BF16).T
        for i, a in enumerate(at):
            dqv[s, :, a : a + hd] = back_low[i * rows : (i + 1) * rows, :]

        scaled_k = dot_nt(u_r, q_low) * kg_row
        back_k = k_inv * (scaled_k - k_n * jnp.mean(scaled_k * k_n, axis=-1, keepdims=True))
        drkv[s, :, h * hd : (h + 1) * hd] = back_k.astype(BF16)
        drvv[s, :, h * hd : (h + 1) * hd] = dot_nt(p_r, g_low).astype(BF16)
        for c in range(pre // block):
            part = pl.ds(c * block, block)
            ck[s, part, :] = ck[prev, part, :] + dot_nt(ub[u, part, :], q_low)
            cv[s, part, :] = cv[prev, part, :] + dot_nt(eb[u, part, :], g_low)

    def run_head(h, events):
        def step(i, carry):
            for at, event in events:
                pl.when(i == at)(event)
            for u in range(2):
                slot_pass(2 * i + u, h, u)
            return carry

        lax.fori_loop(0, slots // 2, step, 0)

    answer()
    own_hat(0)
    enter()
    ag_direct(0)
    greet_far()
    own_hat(1)
    ag_forward(0)
    ag_direct(1)
    for h in range(2, heads):
        own_hat(h)

    for copy in small_loads[1:]:
        copy.wait()
    qg_row = gains[8:9, :]
    rels = []
    for s in range(slots):
        rel = owners[prompts[s]] - me
        rel = jnp.where(rel < 0, rel + n_branch, rel)
        prev = jnp.int32(slots)
        for before in range(s):
            prev = jnp.where(rels[before] == rel, before, prev)
        rels.append(rel)
        meta[0, s] = rel
        meta[1, s] = prev
    for r in range(1, n_branch):
        last = jnp.int32(slots)
        for s in range(slots):
            last = jnp.where(rels[s] == r, s, last)
        meta[2, r] = last
    ck[slots] = jnp.zeros((pre, hd), F32)
    cv[slots] = jnp.zeros((pre, hd), F32)
    gq[...] = jnp.broadcast_to(qg_row, (cols, hd)).T
    gacc[...] = jnp.zeros_like(gacc)
    for copy in rest_loads:
        copy.wait()

    def gather_next(h):
        ag_forward(h)
        if h + 1 < heads:
            ag_direct(h + 1)
        else:
            for done in range(h - 1):
                rs_start(done)

    for h in range(heads):
        ag_rest(h)
        transposes(h)
        if h + 1 < heads:
            events = [(1, functools.partial(gather_next, h + 1))]
        else:
            events = [(2, functools.partial(rs_second, 0))]
        run_head(h, events)
        if h + 1 < heads:
            rs_pack(h)

    for i in range(2):
        ex1[me, i : i + 1, :] = jnp.sum(gacc[i].T, axis=0, keepdims=True)
    ex1[me, 2:8, :] = jnp.zeros((6, hd), F32)

    def gain_copy(src, dst, i, k, j, to):
        return pltpu.make_async_remote_copy(
            src_ref=src, dst_ref=dst, send_sem=gx_send.at[i, k], recv_sem=gx_recv.at[i, j],
            device_id=to, device_id_type=MESH,
        )

    def up(place):
        return gain_copy(ex1.at[place], ex1.at[place], 0, 0, place, {"branch": 0})

    def down(k):
        return gain_copy(ex4, ex4, 3, k, 0, {"branch": k})

    def across(i, k):
        buf, place, _, partner = stages[i]
        return gain_copy(buf.at[place], buf.at[place], 1 + i, k, k, partner(k))

    def collect(buf, extent, copies):
        for copy in copies:
            copy.wait_recv()
        value = buf[0]
        for k in range(1, extent):
            value = value + buf[k]
        return value

    def send_across(i, value):
        buf, place, extent, _ = stages[i]
        buf[place] = value
        for k in range(1, extent):
            across(i, k).start()

    def collect_across(i):
        buf, _, extent, _ = stages[i]
        return collect(buf, extent, [across(i, k) for k in range(1, extent)])

    @pl.when(me != 0)
    def _():
        up(me).start()

    rs_second(heads - 3)
    rs_start(heads - 2)
    rs_pack(heads - 1)
    rs_start(heads - 1)

    @pl.when(me == 0)
    def _():
        value = collect(ex1, n_branch, [up(k) for k in range(1, n_branch)])
        pl.semaphore_wait(barrier, met)
        send_across(0, value)

    rs_final(heads - 4)
    rs_second(heads - 2)

    @pl.when(me == 0)
    def _():
        send_across(1, collect_across(0))

    rs_final(heads - 3)
    rs_second(heads - 1)

    @pl.when(me == 0)
    def _():
        ex4[...] = collect_across(1)
        pl.semaphore_wait(ready.at[1], 1)
        for k in range(1, n_branch):
            down(k).start()

    rs_final(heads - 2)
    rs_final(heads - 1)

    @pl.when(me != 0)
    def _():
        down(me).wait_recv()

    qg_out[...] = ex4[0:1, :]
    kg_out[...] = ex4[1:2, :] / kg_row

    for h in range(heads):
        for i in range(6):
            ag(h, i).wait_send()
            rs(h, i).wait_send()

    @pl.when(me != 0)
    def _():
        up(me).wait_send()

    @pl.when(me == 0)
    def _():
        for i, (_, _, extent, _) in enumerate(stages):
            for k in range(1, extent):
                across(i, k).wait_send()
        for k in range(1, n_branch):
            down(k).wait_send()


def write_out(*refs):
    count = (len(refs) - 3) // 2
    held, last, outs, own, sems = refs[:count], refs[count], refs[count + 1 : -2], refs[-2], refs[-1]
    early = held[4].shape[1] - own.shape[1]
    pairs = list(zip(held, outs))
    pairs[4] = (held[4].at[:, pl.ds(0, early)], outs[4].at[:, pl.ds(0, early)])
    copies = [pltpu.make_async_copy(a, b, sems.at[i]) for i, (a, b) in enumerate(pairs)]
    for copy in copies:
        copy.start()
    own[...] = norm_back(last[0], last[1]).astype(BF16)
    copies.append(
        pltpu.make_async_copy(own, outs[4].at[:, pl.ds(early, own.shape[1])], sems.at[count])
    )
    copies[-1].start()
    for copy in copies:
        copy.wait()


def body(
    n_dp, n_branch,
    prefix_keys, prefix_values, resp_query, resp_keys, resp_values, out_grad,
    q_gain, k_gain, lengths, slot_prompt, prefix_owner,
):
    hd = q_gain.shape[0]
    pre, kvw = prefix_keys.shape[2:]
    slots, rows, qw = resp_query.shape[2:]
    heads = kvw // hd
    group = qw // kvw
    inner = math.gcd(n_dp, 8)
    outer = n_dp // inner
    cols = group * rows
    hbm = pl.BlockSpec(memory_space=pltpu.HBM)
    vmem = pl.BlockSpec(memory_space=pltpu.VMEM)

    def held(dtype, *shape):
        return pltpu.VMEM(shape, dtype)

    prefix_slots = [held(BF16, n_branch, pre, hd) for _ in range(2 * heads)]
    shapes = (
        ((slots, rows, qw), BF16),
        ((slots, rows, qw), BF16),
        ((slots, rows, kvw), BF16),
        ((slots, rows, kvw), BF16),
        ((pre, kvw), BF16),
        ((pre, kvw), BF16),
        ((1, hd), F32),
        ((1, hd), F32),
    )
    results = pl.pallas_call(
        functools.partial(kernel, (n_dp, n_branch, inner, slots, rows, heads, group, pre, hd)),
        out_shape=tuple(pltpu.VMEM(*x) for x in shapes) + (pltpu.VMEM((2, pre, hd), F32),),
        in_specs=[hbm] * 11,
        out_specs=(vmem,) * 9,
        scratch_shapes=[
            held(BF16, slots, rows, qw),
            held(BF16, slots, rows, qw),
            held(BF16, slots, rows, kvw),
            held(BF16, slots, rows, kvw),
            held(BF16, heads, pre, hd),
            *prefix_slots,
            held(BF16, n_branch, hd, pre),
            held(BF16, n_branch, hd, pre),
            held(F32, slots + 1, pre, hd),
            held(F32, slots + 1, pre, hd),
            held(F32, 2, pre, cols),
            held(F32, 2, pre, cols),
            held(BF16, 2, pre, cols),
            held(BF16, 2, pre, cols),
            held(F32, hd, cols),
            held(F32, 2, hd, cols),
            held(BF16, heads, 6, pre, hd),
            held(BF16, heads, 6, pre, hd),
            held(F32, n_branch, 8, hd),
            held(F32, inner, 8, hd),
            held(F32, outer, 8, hd),
            held(F32, 8, hd),
            held(F32, 16, hd),
            pltpu.SMEM((slots,), jnp.int32),
            pltpu.SMEM((slots,), jnp.int32),
            pltpu.SMEM((n_branch,), jnp.int32),
            pltpu.SMEM((3, slots), jnp.int32),
            pltpu.SemaphoreType.DMA((heads, 6)),
            pltpu.SemaphoreType.DMA((heads, 6)),
            pltpu.SemaphoreType.DMA((heads, 6)),
            pltpu.SemaphoreType.DMA((heads, 6)),
            pltpu.SemaphoreType.DMA((4, 8)),
            pltpu.SemaphoreType.DMA((4, 8)),
            pltpu.SemaphoreType.DMA((2 * heads + 9,)),
            pltpu.SemaphoreType.REGULAR((2,)),
        ],
        compiler_params=pltpu.CompilerParams(
            collective_id=0, has_side_effects=True, vmem_limit_bytes=57 * 1024 * 1024
        ),
    )(
        prefix_keys[0, 0], prefix_values[0, 0], resp_query[0, 0], resp_keys[0, 0],
        resp_values[0, 0], out_grad[0, 0], q_gain[None], k_gain[None],
        lengths[0, 0], slot_prompt[0, 0], prefix_owner[0],
    )
    outs = pl.pallas_call(
        write_out,
        out_shape=tuple(jax.ShapeDtypeStruct(*x) for x in shapes),
        in_specs=[vmem] * 9,
        out_specs=(hbm,) * 8,
        scratch_shapes=[held(BF16, pre, hd), pltpu.SemaphoreType.DMA((9,))],
        compiler_params=pltpu.CompilerParams(vmem_limit_bytes=4 * 1024 * 1024),
    )(*results)
    return tuple(x[None, None] for x in outs[:6]) + (outs[6][0], outs[7][0])


def solution(mesh):
    block = P("dp", "branch")
    return jax.shard_map(
        functools.partial(body, mesh.shape["dp"], mesh.shape["branch"]),
        mesh=mesh,
        in_specs=(block,) * 6 + (P(), P()) + (block, block, P("dp")),
        out_specs=(block,) * 6 + (P(), P()),
        check_vma=False,
    )
```

```python
import functools
import math

import jax
import jax.numpy as jnp
from jax import lax
from jax.experimental import pallas as pl
from jax.experimental.pallas import tpu as pltpu
from jax.sharding import PartitionSpec as P

EPSILON = 1e-06
MESH = pl.DeviceIdType.MESH
F32 = jnp.float32
BF16 = jnp.bfloat16
LOG2E = math.log2(math.e)


def dot(a, b):
    return lax.dot_general(a, b, (((1,), (0,)), ((), ())), preferred_element_type=F32)


def dot_nt(a, b):
    return lax.dot_general(a, b, (((1,), (1,)), ((), ())), preferred_element_type=F32)


def norm_parts(raw):
    vals = raw.astype(F32)
    inv = lax.rsqrt(jnp.mean(vals * vals, axis=-1, keepdims=True) + EPSILON)
    return vals * inv, inv


def norm_back(scaled, normed):
    return scaled - normed * jnp.mean(scaled * normed, axis=-1, keepdims=True)


def kernel(
    dims,
    pk, pv, q, rk, rv, g, q_gain, k_gain, lengths_in, prompts_in, owners_in,
    attv, dqv, drkv, drvv, dpk, dpv, qg_out, kg_out, tail,
    qv, gv, rkv, rvv, kraw,
    kb0, kb1, kb2, kb3, vb0, vb1, vb2, vb3,
    kt, vt, ck, cv, es, ds, eb, ub, gq, gacc, rs_out, rs_in, ex1, ex2, ex3, ex4, gains, lengths, prompts, owners, meta,
    ag_send, ag_recv, rs_send, rs_recv, gx_send, gx_recv, load_sem, ready,
):
    n_dp, n_branch, inner, slots, rows, heads, group, pre, hd = dims
    outer = n_dp // inner
    kb, vb = (kb0, kb1, kb2, kb3), (vb0, vb1, vb2, vb3)
    width = group * hd
    cols = group * rows
    score_scale = 1.0 / math.sqrt(hd)

    me = lax.axis_index("branch")
    dp = lax.axis_index("dp")
    right = lax.rem(me + 1, n_branch)
    left = lax.rem(me + n_branch - 1, n_branch)
    in_c = lax.rem(dp, inner)
    out_c = dp // inner
    stages = (
        (ex2, in_c, inner, lambda k: {"dp": out_c * inner + lax.rem(in_c + k, inner)}),
        (ex3, out_c, outer, lambda k: {"dp": lax.rem(out_c + k, outer) * inner + in_c}),
    )
    met = inner + outer - 2

    barrier = pltpu.get_barrier_semaphore()

    def tell(sem, to):
        pl.semaphore_signal(sem, inc=1, device_id=to, device_id_type=MESH)

    @pl.when((me == 1) | (me == 3))
    def _():
        tell(barrier, {"branch": 2})

    @pl.when(me == 0)
    def _():
        for k in (1, 3, 2):
            tell(barrier, {"branch": k})

    def greet_far():
        @pl.when(me == 0)
        def _():
            for _, _, extent, partner in stages:
                for k in range(1, extent):
                    tell(barrier, partner(k))

    def answer():
        @pl.when(me == 2)
        def _():
            pl.semaphore_wait(barrier, 3)
            for k in (1, 3):
                tell(ready.at[0], {"branch": k})
            tell(ready.at[1], {"branch": 0})

        @pl.when((me == 1) | (me == 3))
        def _():
            pl.semaphore_wait(barrier, 1)
            tell(ready.at[0], {"branch": 0})

    def head_cols(h):
        return pl.ds(h * hd, hd)

    k_loads = [
        pltpu.make_async_copy(pk.at[:, head_cols(h)], kraw.at[h], load_sem.at[h])
        for h in range(heads)
    ]
    v_loads = [
        pltpu.make_async_copy(pv.at[:, head_cols(h)], vb[h].at[0], load_sem.at[heads + h])
        for h in range(heads)
    ]
    base = 2 * heads
    rest_loads = [
        pltpu.make_async_copy(src, dst, load_sem.at[base + i])
        for i, (src, dst) in enumerate(((q, qv), (g, gv), (rk, rkv), (rv, rvv)))
    ]
    small_loads = [
        pltpu.make_async_copy(src, dst, load_sem.at[base + 4 + i])
        for i, (src, dst) in enumerate(
            (
                (k_gain, gains.at[pl.ds(0, 1)]),
                (q_gain, gains.at[pl.ds(8, 1)]),
                (lengths_in, lengths),
                (prompts_in, prompts),
                (owners_in, owners),
            )
        )
    ]
    k_loads[0].start()
    small_loads[0].start()
    v_loads[0].start()
    for copy in small_loads[1:]:
        copy.start()
    for h in range(1, heads):
        k_loads[h].start()
        v_loads[h].start()
    for copy in rest_loads:
        copy.start()
    small_loads[0].wait()
    kg_row = gains[0:1, :]

    def own_hat(h):
        k_loads[h].wait()
        normed, _ = norm_parts(kraw[h])
        kb[h][0] = (normed * kg_row).astype(BF16)
        v_loads[h].wait()

    def remote(src, dst, send, recv, to):
        return pltpu.make_async_remote_copy(
            src_ref=src, dst_ref=dst, send_sem=send, recv_sem=recv,
            device_id={"branch": to}, device_id_type=MESH,
        )

    def ag(h, i):
        src, dst, to = (
            (kb[h].at[0], kb[h].at[3], right),
            (vb[h].at[0], vb[h].at[1], left),
            (vb[h].at[0], vb[h].at[3], right),
            (kb[h].at[0], kb[h].at[1], left),
            (kb[h].at[3], kb[h].at[2], right),
            (vb[h].at[1], vb[h].at[2], left),
        )[i]
        return remote(src, dst, ag_send.at[h, i], ag_recv.at[h, i], to)

    def ag_direct(h, parts=(0, 1, 2, 3)):
        for i in parts:
            ag(h, i).start()

    def ag_enter():
        @pl.when(me == 0)
        def _():
            pl.semaphore_wait(ready.at[0], 2)

        @pl.when(me == 1)
        def _():
            ag_direct(0, (1, 3))
            pl.semaphore_wait(ready.at[0], 1)
            ag_direct(0, (0, 2))

        @pl.when(me == 3)
        def _():
            ag_direct(0, (0, 2))
            pl.semaphore_wait(ready.at[0], 1)
            ag_direct(0, (1, 3))

        @pl.when((me == 0) | (me == 2))
        def _():
            ag_direct(0)

    def ag_forward(h):
        ag(h, 0).wait_recv()
        ag(h, 4).start()
        ag(h, 1).wait_recv()
        ag(h, 5).start()

    def ag_rest(h):
        for i in range(2, 6):
            ag(h, i).wait_recv()

    def rs(h, i):
        to = right if i % 2 == 0 else left
        part = pl.ds(2 * i, 2) if i < 2 else i + 2
        return remote(rs_out.at[h, part], rs_in.at[h, part], rs_send.at[h, i], rs_recv.at[h, i], to)

    def rs_pack(h):
        for i, (acc, r) in enumerate(((ck, 2), (cv, 1), (cv, 2), (ck, 3), (ck, 1), (cv, 3))):
            rs_out[h, i] = acc[meta[2, r]].astype(BF16)

    def rs_start(h):
        for i in range(2):
            rs(h, i).start()

    def rs_second(h):
        for i in (0, 1):
            rs(h, i).wait_recv()
            rs_out[h, 4 + i] = (
                rs_out[h, 4 + i].astype(F32) + rs_in[h, 2 * i].astype(F32)
            ).astype(BF16)
            rs(h, 2 + i).start()

    def rs_final(h):
        normed, inv = norm_parts(kraw[h])
        if h == heads - 1:
            tail[1] = normed
        for i in range(2, 4):
            rs(h, i).wait_recv()
        scaled = (rs_in[h, 3].astype(F32) + rs_in[h, 4].astype(F32)) * (inv * kg_row)
        if h == heads - 1:
            tail[0] = scaled
        else:
            dpk[:, h * hd : (h + 1) * hd] = norm_back(scaled, normed).astype(BF16)
        dpv[:, h * hd : (h + 1) * hd] = (rs_in[h, 1].astype(F32) + rs_in[h, 5].astype(F32)).astype(BF16)

    def transposes(h):
        for r in range(1, n_branch):
            kt[r] = kb[h][r].T
            vt[r] = vb[h][r].T

    block = 128
    lane = lax.broadcasted_iota(jnp.int32, (1, cols), 1)
    token = lane & (rows - 1)

    def slot_pass(s, h, u):
        rel = meta[0, s]
        prev = meta[1, s]
        live = token < lengths[s]
        at = [h * width + i * hd for i in range(group)]
        q_t = jnp.concatenate([qv[s, :, a : a + hd] for a in at], axis=0).T.astype(F32)
        g_t = jnp.concatenate([gv[s, :, a : a + hd] for a in at], axis=0).T.astype(F32)
        g_t = jnp.where(live, g_t, 0.0)
        g_low = g_t.astype(BF16)
        q_inv = lax.rsqrt(jnp.mean(q_t * q_t, axis=0, keepdims=True) + EPSILON)
        q_n = q_t * q_inv
        gain = gq[...]
        q_low = (q_n * gain).astype(BF16)
        k_n, k_inv = norm_parts(rkv[s, :, h * hd : (h + 1) * hd])
        k_low = (k_n * kg_row).astype(BF16)
        v_low = rvv[s, :, h * hd : (h + 1) * hd]

        allowed = lax.broadcasted_iota(jnp.int32, (rows, cols), 0) <= token
        e_r = jnp.where(allowed, jnp.exp2(dot(k_low, q_low) * (LOG2E * score_scale)), 0.0)
        d_r = dot(v_low, g_low)
        total = jnp.sum(e_r, axis=0, keepdims=True)
        mixed = jnp.sum(e_r * d_r, axis=0, keepdims=True)
        for c in range(pre // block):
            part = pl.ds(c * block, block)
            e_c = jnp.exp2(dot(kb[h][rel, part, :], q_low) * (LOG2E * score_scale))
            d_c = dot(vb[h][rel, part, :], g_low)
            es[u, part, :] = e_c
            ds[u, part, :] = d_c
            total += jnp.sum(e_c, axis=0, keepdims=True)
            mixed += jnp.sum(e_c * d_c, axis=0, keepdims=True)
        inv = 1.0 / total
        mixed = mixed * inv
        scaled_inv = inv * score_scale
        p_r = (e_r * inv).astype(BF16)
        u_r = (e_r * scaled_inv * (d_r - mixed)).astype(BF16)
        for c in range(pre // block):
            part = pl.ds(c * block, block)
            e_c = es[u, part, :]
            eb[u, part, :] = (e_c * inv).astype(BF16)
            ub[u, part, :] = (e_c * scaled_inv * (ds[u, part, :] - mixed)).astype(BF16)

        o_t = dot(vt[rel], eb[u]) + dot(v_low.T, p_r)
        o_low = jnp.where(live, o_t, 0.0).astype(BF16).T
        for i, a in enumerate(at):
            attv[s, :, a : a + hd] = o_low[i * rows : (i + 1) * rows, :]
        dq_t = dot(kt[rel], ub[u]) + dot(k_low.T, u_r)
        gacc[0] += q_n * dq_t
        gacc[1] += q_low.astype(F32) * dq_t
        scaled = gain * dq_t
        back = q_inv * (scaled - q_n * jnp.mean(scaled * q_n, axis=0, keepdims=True))
        back_low = back.astype(BF16).T
        for i, a in enumerate(at):
            dqv[s, :, a : a + hd] = back_low[i * rows : (i + 1) * rows, :]

        scaled_k = dot_nt(u_r, q_low) * kg_row
        back_k = k_inv * (scaled_k - k_n * jnp.mean(scaled_k * k_n, axis=-1, keepdims=True))
        drkv[s, :, h * hd : (h + 1) * hd] = back_k.astype(BF16)
        drvv[s, :, h * hd : (h + 1) * hd] = dot_nt(p_r, g_low).astype(BF16)
        for c in range(pre // block):
            part = pl.ds(c * block, block)
            ck[s, part, :] = ck[prev, part, :] + dot_nt(ub[u, part, :], q_low)
            cv[s, part, :] = cv[prev, part, :] + dot_nt(eb[u, part, :], g_low)

    def run_head(h, events):
        def step(i, carry):
            for at, event in events:
                pl.when(i == at)(event)
            for u in range(2):
                slot_pass(2 * i + u, h, u)
            return carry

        lax.fori_loop(0, slots // 2, step, 0)

    answer()
    own_hat(0)
    ag_enter()
    greet_far()
    own_hat(1)
    ag_forward(0)
    ag_direct(1)
    for h in range(2, heads):
        own_hat(h)

    for copy in small_loads[1:]:
        copy.wait()
    qg_row = gains[8:9, :]
    rels = []
    for s in range(slots):
        rel = owners[prompts[s]] - me
        rel = jnp.where(rel < 0, rel + n_branch, rel)
        prev = jnp.int32(slots)
        for before in range(s):
            prev = jnp.where(rels[before] == rel, before, prev)
        rels.append(rel)
        meta[0, s] = rel
        meta[1, s] = prev
    for r in range(1, n_branch):
        last = jnp.int32(slots)
        for s in range(slots):
            last = jnp.where(rels[s] == r, s, last)
        meta[2, r] = last
    ck[slots] = jnp.zeros((pre, hd), F32)
    cv[slots] = jnp.zeros((pre, hd), F32)
    gq[...] = jnp.broadcast_to(qg_row, (cols, hd)).T
    gacc[...] = jnp.zeros_like(gacc)
    for copy in rest_loads:
        copy.wait()

    def gather_next(h):
        ag_forward(h)
        if h + 1 < heads:
            ag_direct(h + 1)
        else:
            for done in range(h - 1):
                rs_start(done)

    for h in range(heads):
        ag_rest(h)
        transposes(h)
        if h + 1 < heads:
            events = [(1, functools.partial(gather_next, h + 1))]
        else:
            events = [(2, functools.partial(rs_second, 0))]
        run_head(h, events)
        if h + 1 < heads:
            rs_pack(h)

    for i in range(2):
        ex1[me, i : i + 1, :] = jnp.sum(gacc[i].T, axis=0, keepdims=True)
    ex1[me, 2:8, :] = jnp.zeros((6, hd), F32)

    def gain_copy(src, dst, i, k, j, to):
        return pltpu.make_async_remote_copy(
            src_ref=src, dst_ref=dst, send_sem=gx_send.at[i, k], recv_sem=gx_recv.at[i, j],
            device_id=to, device_id_type=MESH,
        )

    def up(place):
        return gain_copy(ex1.at[place], ex1.at[place], 0, 0, place, {"branch": 0})

    def down(k):
        return gain_copy(ex4, ex4, 3, k, 0, {"branch": k})

    def across(i, k):
        buf, place, _, partner = stages[i]
        return gain_copy(buf.at[place], buf.at[place], 1 + i, k, k, partner(k))

    def collect(buf, extent, copies):
        for copy in copies:
            copy.wait_recv()
        value = buf[0]
        for k in range(1, extent):
            value = value + buf[k]
        return value

    def send_across(i, value):
        buf, place, extent, _ = stages[i]
        buf[place] = value
        for k in range(1, extent):
            across(i, k).start()

    def collect_across(i):
        buf, _, extent, _ = stages[i]
        return collect(buf, extent, [across(i, k) for k in range(1, extent)])

    @pl.when(me != 0)
    def _():
        up(me).start()

    rs_second(heads - 3)
    rs_start(heads - 2)
    rs_pack(heads - 1)
    rs_start(heads - 1)

    @pl.when(me == 0)
    def _():
        value = collect(ex1, n_branch, [up(k) for k in range(1, n_branch)])
        pl.semaphore_wait(barrier, met)
        send_across(0, value)

    rs_final(heads - 4)
    rs_second(heads - 2)

    @pl.when(me == 0)
    def _():
        send_across(1, collect_across(0))

    rs_final(heads - 3)
    rs_second(heads - 1)

    @pl.when(me == 0)
    def _():
        ex4[...] = collect_across(1)
        pl.semaphore_wait(ready.at[1], 1)
        for k in range(1, n_branch):
            down(k).start()

    rs_final(heads - 2)
    rs_final(heads - 1)

    @pl.when(me != 0)
    def _():
        down(me).wait_recv()

    qg_out[...] = ex4[0:1, :]
    kg_out[...] = ex4[1:2, :] / kg_row

    for h in range(heads):
        for i in range(6):
            ag(h, i).wait_send()
        for i in range(4):
            rs(h, i).wait_send()

    @pl.when(me != 0)
    def _():
        up(me).wait_send()

    @pl.when(me == 0)
    def _():
        for i, (_, _, extent, _) in enumerate(stages):
            for k in range(1, extent):
                across(i, k).wait_send()
        for k in range(1, n_branch):
            down(k).wait_send()


def write_out(*refs):
    count = (len(refs) - 3) // 2
    held, last, outs, own, sems = refs[:count], refs[count], refs[count + 1 : -2], refs[-2], refs[-1]
    early = held[4].shape[1] - own.shape[1]
    pairs = list(zip(held, outs))
    pairs[4] = (held[4].at[:, pl.ds(0, early)], outs[4].at[:, pl.ds(0, early)])
    copies = [pltpu.make_async_copy(a, b, sems.at[i]) for i, (a, b) in enumerate(pairs)]
    for copy in copies:
        copy.start()
    own[...] = norm_back(last[0], last[1]).astype(BF16)
    copies.append(
        pltpu.make_async_copy(own, outs[4].at[:, pl.ds(early, own.shape[1])], sems.at[count])
    )
    copies[-1].start()
    for copy in copies:
        copy.wait()


def body(
    n_dp, n_branch,
    prefix_keys, prefix_values, resp_query, resp_keys, resp_values, out_grad,
    q_gain, k_gain, lengths, slot_prompt, prefix_owner,
):
    hd = q_gain.shape[0]
    pre, kvw = prefix_keys.shape[2:]
    slots, rows, qw = resp_query.shape[2:]
    heads = kvw // hd
    group = qw // kvw
    inner = math.gcd(n_dp, 8)
    outer = n_dp // inner
    cols = group * rows
    hbm = pl.BlockSpec(memory_space=pltpu.HBM)
    vmem = pl.BlockSpec(memory_space=pltpu.VMEM)

    def held(dtype, *shape):
        return pltpu.VMEM(shape, dtype)

    prefix_slots = [held(BF16, n_branch, pre, hd) for _ in range(2 * heads)]
    shapes = (
        ((slots, rows, qw), BF16),
        ((slots, rows, qw), BF16),
        ((slots, rows, kvw), BF16),
        ((slots, rows, kvw), BF16),
        ((pre, kvw), BF16),
        ((pre, kvw), BF16),
        ((1, hd), F32),
        ((1, hd), F32),
    )
    results = pl.pallas_call(
        functools.partial(kernel, (n_dp, n_branch, inner, slots, rows, heads, group, pre, hd)),
        out_shape=tuple(pltpu.VMEM(*x) for x in shapes) + (pltpu.VMEM((2, pre, hd), F32),),
        in_specs=[hbm] * 11,
        out_specs=(vmem,) * 9,
        scratch_shapes=[
            held(BF16, slots, rows, qw),
            held(BF16, slots, rows, qw),
            held(BF16, slots, rows, kvw),
            held(BF16, slots, rows, kvw),
            held(BF16, heads, pre, hd),
            *prefix_slots,
            held(BF16, n_branch, hd, pre),
            held(BF16, n_branch, hd, pre),
            held(F32, slots + 1, pre, hd),
            held(F32, slots + 1, pre, hd),
            held(F32, 2, pre, cols),
            held(F32, 2, pre, cols),
            held(BF16, 2, pre, cols),
            held(BF16, 2, pre, cols),
            held(F32, hd, cols),
            held(F32, 2, hd, cols),
            held(BF16, heads, 6, pre, hd),
            held(BF16, heads, 6, pre, hd),
            held(F32, n_branch, 8, hd),
            held(F32, inner, 8, hd),
            held(F32, outer, 8, hd),
            held(F32, 8, hd),
            held(F32, 16, hd),
            pltpu.SMEM((slots,), jnp.int32),
            pltpu.SMEM((slots,), jnp.int32),
            pltpu.SMEM((n_branch,), jnp.int32),
            pltpu.SMEM((3, slots), jnp.int32),
            pltpu.SemaphoreType.DMA((heads, 6)),
            pltpu.SemaphoreType.DMA((heads, 6)),
            pltpu.SemaphoreType.DMA((heads, 6)),
            pltpu.SemaphoreType.DMA((heads, 6)),
            pltpu.SemaphoreType.DMA((4, 8)),
            pltpu.SemaphoreType.DMA((4, 8)),
            pltpu.SemaphoreType.DMA((2 * heads + 9,)),
            pltpu.SemaphoreType.REGULAR((2,)),
        ],
        compiler_params=pltpu.CompilerParams(
            collective_id=0, has_side_effects=True, vmem_limit_bytes=57 * 1024 * 1024
        ),
    )(
        prefix_keys[0, 0], prefix_values[0, 0], resp_query[0, 0], resp_keys[0, 0],
        resp_values[0, 0], out_grad[0, 0], q_gain[None], k_gain[None],
        lengths[0, 0], slot_prompt[0, 0], prefix_owner[0],
    )
    outs = pl.pallas_call(
        write_out,
        out_shape=tuple(jax.ShapeDtypeStruct(*x) for x in shapes),
        in_specs=[vmem] * 9,
        out_specs=(hbm,) * 8,
        scratch_shapes=[held(BF16, pre, hd), pltpu.SemaphoreType.DMA((9,))],
        compiler_params=pltpu.CompilerParams(vmem_limit_bytes=4 * 1024 * 1024),
    )(*results)
    return tuple(x[None, None] for x in outs[:6]) + (outs[6][0], outs[7][0])


def solution(mesh):
    block = P("dp", "branch")
    return jax.shard_map(
        functools.partial(body, mesh.shape["dp"], mesh.shape["branch"]),
        mesh=mesh,
        in_specs=(block,) * 6 + (P(), P()) + (block, block, P("dp")),
        out_specs=(block,) * 6 + (P(), P()),
        check_vma=False,
    )
```
